32 devices in a mesh: grp: 4 (over x, core), sub: 8 (over z, y).
Axes of the slice: x: 2, y: 2, z: 4, core: 2. Of those that a mesh axis runs over, the one named last changes fastest.
Arguments:
- right_side: float32 [65536, 128], P(('grp', 'sub')), may hold values from -6 to 6
- fine_values: float32 [81, 65536], P(None, ('grp', 'sub')), as said below
- columns: int32 [81, 65536], P(None, ('grp', 'sub')), may hold values from 0 to 2175, as said below
- agg_map: int32 [65536], P(('grp', 'sub')), may hold values from 0 to 127
- send_lo: int32 [2048], P(('grp', 'sub')), may hold values from 0 to 2047
- send_hi: int32 [2048], P(('grp', 'sub')), may hold values from 0 to 2047
- coarse_matrix: float32 [4, 1024, 1024], P('grp', 'sub'), as said below
Outputs:
- solution: float32 [65536, 128], P(('grp', 'sub'))
- residual: float32 [65536, 128], P(('grp', 'sub'))
The draws below stay inside these ranges and needn't reach their ends.
Inputs may be any that keep to these rules, and one draw needn't show every extreme that they name: `columns`: entry 0 of row i of a partition is 64 + i, the others lie within 64 positions of it. `fine_values`: entry 0 lies in 2.5 to 5 and every other entry's magnitude is at most 0.06. `coarse_matrix`: symmetric; the diagonal lies in 10 to 20, other entries' magnitudes are at most 7.1 / sqrt(1024).
All inputs are finite; a program needn't handle non-finite values.
Results may differ from the reference program's by a relative error of at most 0.0001.
Values sent between devices are 32-bit elements; how exact they have to be, the bound alone decides.
A program may use at most 128 MiB of HBM per device.

```python
import jax
import jax.numpy as jnp
from jax import lax

ROWS_DEV = 2048
NRHS = 128
STENCIL = 81
GHOST = 64
AGG_SIZE = 16
CHEB_FINE = 2
CHEB_COARSE = 6
CYCLES = 2
BLOCK = 128
AGG = 128
COARSE = 1024
ROWS = 65536
N_GRP = 4
DEVICES = 32


def draw_columns(key, part):
    rows = jnp.arange(ROWS, dtype=jnp.int32) % ROWS_DEV
    offsets = jax.random.randint(key, (STENCIL, ROWS), -GHOST, GHOST + 1, dtype=jnp.int32)
    entry = jnp.arange(STENCIL, dtype=jnp.int32)[:, None]
    offsets = jnp.where(entry == 0, 0, offsets)
    offsets = jnp.where((entry == 1) & (rows[None, :] == 0), -GHOST, offsets)
    offsets = jnp.where((entry == 1) & (rows[None, :] == ROWS_DEV - 1), GHOST, offsets)
    return (GHOST + rows[None, :] + offsets).astype(jnp.int32)


def draw_fine_values(key, part):
    diagonal = jax.random.uniform(jax.random.fold_in(key, 1), (1, ROWS), jnp.float32, 2.5, 5.0)
    others = jax.random.uniform(jax.random.fold_in(key, 2), (STENCIL, ROWS), jnp.float32, -0.06, 0.06)
    entry = jnp.arange(STENCIL, dtype=jnp.int32)[:, None]
    return jnp.where(entry == 0, diagonal, others)


def draw_agg_map(key, part):
    rows = jnp.arange(ROWS, dtype=jnp.int32) % ROWS_DEV
    base = rows // AGG_SIZE
    moved = jax.random.randint(jax.random.fold_in(key, 3), (ROWS,), 0, AGG, dtype=jnp.int32)
    select = jax.random.randint(jax.random.fold_in(key, 4), (ROWS,), 0, 4, dtype=jnp.int32)
    return jnp.where(select == 0, moved, base).astype(jnp.int32)


def draw_coarse_matrix(key, part):
    bound = 5.0 / jnp.sqrt(jnp.float32(COARSE))
    table = jax.random.uniform(jax.random.fold_in(key, 5), (N_GRP, COARSE, COARSE), jnp.float32, -1.0, 1.0) * bound
    others = (table + jnp.swapaxes(table, 1, 2)) * 0.70710677
    diagonal = jax.random.uniform(jax.random.fold_in(key, 6), (N_GRP, COARSE, 1), jnp.float32, 10.0, 20.0)
    rows = jnp.arange(COARSE, dtype=jnp.int32)
    same = rows[:, None] == rows[None, :]
    return jnp.where(same[None, :, :], diagonal, others)


def place_ends(values, key, least, top_value):
    longest = values.shape.index(max(values.shape))
    spots = []
    for shift in (0, 1):
        where = [jax.random.randint(jax.random.fold_in(key, axis), (), 0, length) for axis, length in enumerate(values.shape)]
        where[longest] = (where[longest] + shift) % values.shape[longest]
        spots.append(tuple(where))
    return values.at[spots[0]].set(least).at[spots[1]].set(top_value)


def block_levels(rng, shape, cuts, low, largest):
    loudness = 1.0
    for axis_at, blocks in cuts:
        draws = jax.random.uniform(jax.random.fold_in(jax.random.fold_in(rng, 6), axis_at), (blocks,), jnp.float32, low / len(cuts), largest / len(cuts))
        loudness = loudness * jnp.repeat(jnp.exp(draws), shape[axis_at] // blocks).reshape((-1,) + (1,) * (len(shape) - 1 - axis_at))
    return loudness


def normal_values(stream_key, shape, scale, most, split=(), kind=jnp.bfloat16):
    gain = block_levels(stream_key, shape, split, -0.22, 0.18) if split else 1.0
    entries = jax.random.normal(stream_key, shape, jnp.float32) * scale * gain
    return jnp.minimum(jnp.maximum(entries, -most), most).astype(kind)


def setup_inputs(seed: int = 0) -> dict:
    streams_of = jax.random.split(jax.random.key(seed), 8)
    right_side = normal_values(streams_of[0], (ROWS, NRHS), 1.0, 6.0, ((0, 32),), jnp.float32)
    fine_values = draw_fine_values(jax.random.fold_in(streams_of[7], 71), 0)
    columns = draw_columns(jax.random.fold_in(streams_of[7], 71), 0)
    agg_map = draw_agg_map(jax.random.fold_in(streams_of[7], 71), 0)
    send_lo = place_ends(jax.random.randint(streams_of[4], (DEVICES * GHOST,), 0, ROWS_DEV), jax.random.fold_in(streams_of[4], 1), 0, ROWS_DEV - 1).astype(jnp.int32)
    send_hi = place_ends(jax.random.randint(streams_of[5], (DEVICES * GHOST,), 0, ROWS_DEV), jax.random.fold_in(streams_of[5], 1), 0, ROWS_DEV - 1).astype(jnp.int32)
    coarse_matrix = draw_coarse_matrix(jax.random.fold_in(streams_of[7], 71), 0)
    return {"right_side": right_side, "fine_values": fine_values, "columns": columns, "agg_map": agg_map, "send_lo": send_lo, "send_hi": send_hi, "coarse_matrix": coarse_matrix}


THETA = 1.0
DELTA = 0.7
OMEGA = 0.6
highest = lax.Precision.HIGHEST


def picker(table, index):
    return jax.vmap(lambda source, where: jnp.take(source, where, axis=0))(table, index)


def band_tiles(fine_values, columns):
    rows = jnp.arange(ROWS_DEV, dtype=jnp.int32)
    starts = (rows // BLOCK) * BLOCK
    index_all = columns.reshape(STENCIL, DEVICES, ROWS_DEV)
    flat = rows[None, None, :] * (2 * BLOCK) + index_all - starts[None, None, :]
    offsets = jnp.arange(DEVICES, dtype=jnp.int32) * (ROWS_DEV * 2 * BLOCK)
    flat = (flat + offsets[None, :, None]).astype(jnp.int32)
    tiles = jnp.zeros((DEVICES * ROWS_DEV * 2 * BLOCK,), jnp.float32)
    tiles = tiles.at[flat.reshape(-1)].add(fine_values.reshape(-1))
    tiles = tiles.reshape(DEVICES, ROWS_DEV // BLOCK, BLOCK, 2 * BLOCK)
    return tiles[:, :, :, :BLOCK], tiles[:, :, :, BLOCK:]


def fine_apply(vector, low_tiles, high_tiles, send_lo, send_hi):
    blocks = vector.reshape(DEVICES, ROWS_DEV, NRHS)
    upper_rows = picker(blocks, send_hi.reshape(DEVICES, GHOST))
    lower_rows = picker(blocks, send_lo.reshape(DEVICES, GHOST))
    empty = jnp.zeros((1, GHOST, NRHS), jnp.float32)
    below = jnp.concatenate([empty, upper_rows[:-1]], 0)
    above = jnp.concatenate([lower_rows[1:], empty], 0)
    extended = jnp.concatenate([below, blocks, above], 1)
    pieces = extended.reshape(DEVICES, ROWS_DEV // BLOCK + 1, BLOCK, NRHS)
    total = jnp.einsum('dbrc,dbcn->dbrn', low_tiles, pieces[:, :-1], precision=highest)
    total = total + jnp.einsum('dbrc,dbcn->dbrn', high_tiles, pieces[:, 1:], precision=highest)
    return total.reshape(ROWS, NRHS)


def chebyshev(residual, apply, inverse, steps, final):
    rho_old = DELTA / THETA
    direction = inverse * residual / THETA
    result = direction
    for turn in range(1, steps):
        residual = residual - apply(direction)
        rho_new = 1.0 / (2.0 * THETA / DELTA - rho_old)
        direction = rho_new * rho_old * direction + (2.0 * rho_new / DELTA) * inverse * residual
        result = result + direction
        rho_old = rho_new
    if final:
        residual = residual - apply(direction)
    return result, residual


def reference(right_side, fine_values, columns, agg_map, send_lo, send_hi, coarse_matrix):
    low_tiles, high_tiles = band_tiles(fine_values, columns)

    def apply_fine(vector):
        return fine_apply(vector, low_tiles, high_tiles, send_lo, send_hi)

    def apply_coarse(vector):
        return jnp.einsum('gij,gjn->gin', coarse_matrix, vector, precision=highest)

    dinv = 1.0 / fine_values[0][:, None]
    cinv = 1.0 / jnp.diagonal(coarse_matrix, axis1=1, axis2=2)[:, :, None]
    maps = agg_map.reshape(DEVICES, ROWS_DEV)
    onehot = (maps[:, :, None] == jnp.arange(AGG, dtype=jnp.int32)[None, None, :]).astype(jnp.float32)
    solution = jnp.zeros_like(right_side)
    residual = right_side
    for cycle in range(CYCLES):
        update, residual = chebyshev(residual, apply_fine, dinv, CHEB_FINE, True)
        solution = solution + update
        smoothed = residual - OMEGA * apply_fine(dinv * residual)
        coarse_rhs = jnp.einsum('dra,drn->dan', onehot, smoothed.reshape(DEVICES, ROWS_DEV, NRHS), precision=highest)
        coarse_rhs = coarse_rhs.reshape(N_GRP, COARSE, NRHS)
        coarse_corr, unused = chebyshev(coarse_rhs, apply_coarse, cinv, CHEB_COARSE, False)
        spread = picker(coarse_corr.reshape(DEVICES, AGG, NRHS), maps).reshape(ROWS, NRHS)
        correction = spread - OMEGA * dinv * apply_fine(spread)
        solution = solution + correction
        residual = residual - apply_fine(correction)
        update, residual = chebyshev(residual, apply_fine, dinv, CHEB_FINE, True)
        solution = solution + update
    return solution, residual
```

```python
import functools

import jax
import jax.numpy as jnp
from jax import lax
from jax.experimental import pallas as pl
from jax.experimental.pallas import tpu as pltpu
from jax.sharding import PartitionSpec as P

CHEB_COARSE = 6
CYCLES = 2
ROUNDS = 4
CHUNKS = 2

THETA = 1.0
DELTA = 0.7
OMEGA = 0.6
RHO0 = DELTA / THETA
RHO1 = 1.0 / (2.0 * THETA / DELTA - RHO0)
C1 = RHO1 * RHO0
C2 = 2.0 * RHO1 / DELTA
MESH = pl.DeviceIdType.MESH
f32 = jnp.float32
bf16 = jnp.bfloat16


def split(x):
    hi = x.astype(bf16)
    lo = (x - hi.astype(f32)).astype(bf16)
    return hi, lo


def split_lanes(x):
    hi, lo = split(x)
    return jnp.concatenate([hi, lo], axis=1)


def iota(shape, dim):
    return lax.broadcasted_iota(jnp.int32, shape, dim)


def dot(a, b):
    return jnp.dot(a, b, preferred_element_type=f32)


def quads(product, rows, width):
    return product[:rows, :width] + (product[:rows, width:] + product[rows:, :width])


def aligned(start, size):
    return pl.ds(pl.multiple_of(start, size), size)


def band_tile(fv_ref, col_ref, b, block):
    groups = (fv_ref.shape[0] - 1) // 8
    sl = aligned(b * block, block)
    rows = iota((8, block), 1) + b * block
    cols, vals, firsts = [], [], []
    for i in range(groups):
        cols.append(col_ref[1 + 8 * i : 9 + 8 * i, sl] - rows)
        vals.append(fv_ref[1 + 8 * i : 9 + 8 * i, sl])
    last = jnp.zeros((8, block), f32)
    for i in range(groups):
        last = last + jnp.where(cols[i] == block, vals[i], 0.0)
    last = jnp.sum(last, axis=0, keepdims=True)
    for j in range(groups):
        total = vals[j]
        for i in range(j + 1, groups):
            total = total + jnp.where(cols[i] == cols[j], vals[i], 0.0)
        firsts.append(total)
    high_count = block // 8
    places = [iota((8, block), 0) + 8 * h for h in range(high_count)]
    sums = [jnp.zeros((8, block), f32)] * high_count
    for s in range(8):
        chains = [jnp.zeros((8, block), f32)] * high_count
        for i in reversed(range(groups)):
            col = jnp.broadcast_to(cols[i][s : s + 1, :], (8, block))
            val = jnp.broadcast_to(firsts[i][s : s + 1, :], (8, block))
            chains = [jnp.where(col == places[h], val, chains[h]) for h in range(high_count)]
        sums = [sums[h] + chains[h] for h in range(high_count)]
    by_offset = jnp.concatenate(sums, axis=0).T
    skewed = pltpu.roll(by_offset, 0, 1, stride=1, stride_axis=0)
    lane = iota((block, block), 1)
    sub = iota((block, block), 0)
    low = jnp.where(lane >= sub, skewed, 0.0)
    high = jnp.where(lane < sub, skewed, jnp.where(lane == sub, last, 0.0))
    return low, high


def kernel(n_grp, n_sub, *refs):
    (rhs_ref, fv_ref, col_ref, agg_ref, lo_ref, hi_ref, own_ref,
     sol_ref, res_ref,
     a2, dinv_ref, diag_ref, oh_ref, oht_ref, g_ref, sa, dinv_s,
     xs, ext_v, ext_w, s2, y_mid,
     send, recv, far, r_send, r_recv, r2,
     send_sem, recv_sem, far_send_sem, far_recv_sem, r_send_sem, r_recv_sem,
     slabs, slab_send_sem, slab_recv_sem, m_hi, m_lo, pd, pz, px, pair2, m2,
     csend, whole, csend_sem, crecv_sem) = refs
    rows_dev, width = rhs_ref.shape
    ghost = lo_ref.shape[1]
    block = 2 * ghost
    blocks = rows_dev // block
    agg, coarse = own_ref.shape
    parts = coarse // agg
    kept = slabs.shape[1]
    grp = lax.axis_index("grp")
    me = lax.axis_index("sub")
    total = n_grp * n_sub
    part = grp * n_sub + me
    ones = functools.partial(jnp.asarray, dtype=jnp.int32)

    def device(p):
        return lax.div(p, n_sub), lax.rem(p, n_sub)

    has = {d: jnp.logical_and(part + d >= 0, part + d < total) for d in (1, -1, 2, -2)}

    barrier = pltpu.get_barrier_semaphore()
    for j in range(1, n_sub):
        pl.semaphore_signal(barrier, inc=1, device_id=(grp, lax.rem(me + j, n_sub)), device_id_type=MESH)
    greeted = n_sub - 1
    for d in (1, -1, 2, -2):
        outside = jnp.logical_or(me + d < 0, me + d >= n_sub)
        across = jnp.logical_and(has[d], outside)

        @pl.when(across)
        def _():
            pl.semaphore_signal(barrier, inc=1, device_id=device(part + d), device_id_type=MESH)

        greeted = greeted + across.astype(jnp.int32)

    mine = aligned(me * agg, agg)
    for k in range(kept // agg):
        slabs[mine, k * agg : (k + 1) * agg] = own_ref[:, aligned(lax.rem(me + k, n_sub) * agg, agg)]
    pl.semaphore_wait(barrier, greeted)

    line = n_sub // 2
    pos = lax.div(me, 2)
    odd = lax.rem(me, 2)
    partner = me + 1 - 2 * odd
    chunk = agg // CHUNKS
    RIGHT, LEFT, ACROSS = 0, 1, 2

    def slab_copy(origin, c, way):
        peer = (me + 2, me - 2, partner)[way]
        at = pl.ds(pl.multiple_of(origin * agg + c * chunk, chunk), chunk)
        return pltpu.make_async_remote_copy(
            src_ref=slabs.at[at], dst_ref=slabs.at[at],
            send_sem=slab_send_sem.at[way, lax.div(origin, 2), c],
            recv_sem=slab_recv_sem.at[way, lax.div(origin, 2), c],
            device_id=(grp, peer), device_id_type=MESH,
        )

    def slab_open():
        for c in range(CHUNKS):
            @pl.when(pos + 1 < line)
            def _():
                slab_copy(me, c, RIGHT).start()

            @pl.when(pos > 0)
            def _():
                slab_copy(me, c, LEFT).start()

            slab_copy(me, c, ACROSS).start()

    def slab_pass(event):
        step = 1 + lax.div(event, CHUNKS)
        c = lax.rem(event, CHUNKS)

        @pl.when(pos - step >= 0)
        def _():
            origin = me - 2 * step
            slab_copy(origin, c, RIGHT).wait_recv()

            @pl.when(pos + 1 < line)
            def _():
                slab_copy(origin, c, RIGHT).start()

            slab_copy(origin, c, ACROSS).start()

        @pl.when(pos + step < line)
        def _():
            origin = me + 2 * step
            slab_copy(origin, c, LEFT).wait_recv()

            @pl.when(pos > 0)
            def _():
                slab_copy(origin, c, LEFT).start()

            slab_copy(origin, c, ACROSS).start()

    def slab_close():
        def one(i, carry):
            q = lax.div(i, CHUNKS)
            c = lax.rem(i, CHUNKS)
            slab_copy(2 * q + 1 - odd, c, ACROSS).wait_recv()
            origin = 2 * q + odd
            slab_copy(origin, c, ACROSS).wait_send()

            @pl.when(jnp.logical_and(q <= pos, pos + 1 < line))
            def _():
                slab_copy(origin, c, RIGHT).wait_send()

            @pl.when(jnp.logical_and(q >= pos, pos > 0))
            def _():
                slab_copy(origin, c, LEFT).wait_send()

            return carry

        lax.fori_loop(0, line * CHUNKS, one, 0)

    events = (line - 1) * CHUNKS
    first_event_block = 4
    in_setup = min(events, blocks - first_event_block)
    slab_open()

    for d, slot in ((-1, 0), (1, 1)):
        @pl.when(jnp.logical_not(has[d]))
        def _():
            recv[:, slot] = jnp.zeros((recv.shape[0],) + recv.shape[2:], f32)
            r_recv[slot] = jnp.zeros(r_recv.shape[1:], f32)

    for d, slot in ((-2, 0), (2, 1)):
        @pl.when(jnp.logical_not(has[d]))
        def _():
            far[:, slot] = jnp.zeros((far.shape[0],) + far.shape[2:], f32)

    for ext in (ext_v, ext_w):
        ext[:ghost, :] = jnp.zeros((ghost, 2 * width), bf16)
        ext[ghost + rows_dev :, :] = jnp.zeros((ghost, 2 * width), bf16)
    sent_row = jnp.concatenate([hi_ref[...], lo_ref[...]], axis=1).astype(f32)
    sent = jnp.broadcast_to(sent_row, (2 * ghost, 2 * ghost)).T.astype(jnp.int32)
    lane = iota((2 * ghost, block), 1)
    for j in range(blocks + 1):
        g_ref[: 2 * ghost, j * block : (j + 1) * block] = (sent + (ghost - j * block) == lane).astype(f32).astype(bf16)
    dinv_s[...] = jnp.zeros_like(dinv_s)
    sa[:, :block] = jnp.zeros((2 * ghost, block), f32)

    def setup(b, carry):
        sl = aligned(b * block, block)
        low, high = band_tile(fv_ref, col_ref, b, block)
        diag = jnp.broadcast_to(fv_ref[0:1, sl], (block, block)).T
        dinv = 1.0 / diag
        diag_ref[sl, :] = diag
        dinv_ref[sl, :] = dinv
        low_hi, low_lo = split(low)
        high_hi, high_lo = split(high)
        hi = jnp.concatenate([low_hi, high_hi], axis=1)
        lo = jnp.concatenate([low_lo, high_lo], axis=1)
        a2[aligned(b * 2 * block, block), :] = hi
        a2[aligned(b * 2 * block + block, block), :] = lo
        onehot = (iota((agg, block), 0) == agg_ref[:, sl]).astype(f32)
        oht_ref[:, sl] = onehot.astype(bf16)
        oh_ref[sl, :] = onehot.T.astype(bf16)
        picked = (sent - b * block == lane).astype(f32).astype(bf16)
        part_sa = dot(picked, hi) + dot(picked, lo)
        sa[:, sl] = sa[:, sl] + part_sa[:, :block]
        sa[:, aligned((b + 1) * block, block)] = part_sa[:, block:]
        both = dot(picked, split_lanes(dinv))
        dinv_s[...] += both[:, :block] + both[:, block:]
        rhs = rhs_ref[sl, :]
        res_ref[sl, :] = rhs
        sol_ref[sl, :] = jnp.zeros_like(rhs)
        v = dinv * rhs
        xs[sl, :] = v
        ext_v[pl.ds(pl.multiple_of(ghost + b * block, ghost), block), :] = split_lanes(v)

        @pl.when(jnp.logical_and(b >= first_event_block, b < first_event_block + in_setup))
        def _():
            slab_pass(b - first_event_block)

        return carry

    lax.fori_loop(0, blocks, setup, 0)
    for j in range(blocks + 1):
        at = slice(j * block, (j + 1) * block)
        scaled = sa[:, at] * dinv_s[...]
        g_ref[2 * ghost : 4 * ghost, at], g_ref[4 * ghost :, at] = split(scaled)
        if j == 0:
            below = scaled
    response = jnp.where(lane < ghost, below, scaled)
    r_send[0] = response[:ghost]
    r_send[1] = response[ghost:]

    def r_copy(way):
        d = (1, -1)[way]
        return pltpu.make_async_remote_copy(
            src_ref=r_send.at[way], dst_ref=r_recv.at[way],
            send_sem=r_send_sem.at[way], recv_sem=r_recv_sem.at[way],
            device_id=device(part + d), device_id_type=MESH,
        )

    def near_copy(ex, way, count):
        d = (1, -1)[way]
        return pltpu.make_async_remote_copy(
            src_ref=send.at[ex, way, pl.ds(0, count)], dst_ref=recv.at[ex, way, pl.ds(0, count)],
            send_sem=send_sem.at[ex, way], recv_sem=recv_sem.at[ex, way],
            device_id=device(part + d), device_id_type=MESH,
        )

    def far_copy(ex, way):
        d = (2, -2)[way]
        return pltpu.make_async_remote_copy(
            src_ref=send.at[ex, way, pl.ds(0, ghost)], dst_ref=far.at[ex, way],
            send_sem=far_send_sem.at[ex, way], recv_sem=far_recv_sem.at[ex, way],
            device_id=device(part + d), device_id_type=MESH,
        )

    def mid_product(double):
        high = 6 * ghost if double else 2 * ghost
        inner = slice(2 * block, (blocks - 1) * block)
        y_mid[:high] = dot(g_ref[:high, inner], ext_v[inner, :])

    def depart(ex, double, alpha, beta):
        high = 6 * ghost if double else 2 * ghost
        y = y_mid[:high]
        for ends in (slice(0, 2 * block), slice((blocks - 1) * block, (blocks + 1) * block)):
            y = y + dot(g_ref[:high, ends], ext_v[ends, :])
        now = y[: 2 * ghost, :width] + y[: 2 * ghost, width:]
        for way in range(2):
            send[ex, way, :ghost] = now[way * ghost : (way + 1) * ghost]
        if double:
            later = alpha * now - beta * quads(y[2 * ghost :], 2 * ghost, width)
            for way in range(2):
                send[ex, way, ghost:] = later[way * ghost : (way + 1) * ghost]
        for way, d in ((0, 1), (1, -1)):
            @pl.when(has[d])
            def _():
                near_copy(ex, way, 2 * ghost if double else ghost).start()
        if double:
            for way, d in ((0, 2), (1, -2)):
                @pl.when(has[d])
                def _():
                    far_copy(ex, way).start()

    def arrive(ex, double):
        count = 2 * ghost if double else ghost
        for way, d in ((0, 1), (1, -1)):
            @pl.when(has[-d])
            def _():
                near_copy(ex, way, count).wait_recv()

            @pl.when(has[d])
            def _():
                near_copy(ex, way, count).wait_send()
        if double:
            for way, d in ((0, 2), (1, -2)):
                @pl.when(has[-d])
                def _():
                    far_copy(ex, way).wait_recv()

                @pl.when(has[d])
                def _():
                    far_copy(ex, way).wait_send()

    def local_apply(ext, fn):
        def go(b, carry):
            a = a2[aligned(b * 2 * block, 2 * block), :]
            x = ext[pl.ds(pl.multiple_of(b * block, block), 2 * block), :]
            fn(b, aligned(b * block, block), quads(dot(a, x), block, width))
            return carry

        lax.fori_loop(0, blocks, go, 0, unroll=4)

    def store_ext(ext, b, x):
        ext[pl.ds(pl.multiple_of(ghost + b * block, ghost), block), :] = split_lanes(x)

    last_tile = (blocks - 1) * 2 * block
    below_rows = slice(0, ghost)
    above_rows = slice(rows_dev - ghost, rows_dev)

    def ghost_terms(ex):
        nothing = jnp.zeros((ghost, 2 * width), bf16)
        a_below = jnp.concatenate([a2[:ghost, :block], a2[block : block + ghost, :block]], axis=0)
        a_above = jnp.concatenate(
            [a2[last_tile + ghost : last_tile + block, block:], a2[last_tile + block + ghost : last_tile + 2 * block, block:]],
            axis=0,
        )
        from_below = jnp.concatenate([split_lanes(recv[ex, 0, :ghost]), nothing], axis=0)
        from_above = jnp.concatenate([nothing, split_lanes(recv[ex, 1, :ghost])], axis=0)
        return quads(dot(a_below, from_below), ghost, width), quads(dot(a_above, from_above), ghost, width)

    def pair(ex, te):
        alpha, beta = (1.0 - OMEGA, OMEGA) if te else (C1, C2)
        gamma = OMEGA if te else C2 - 1.0
        depart(ex, True, alpha, beta)

        def first(b, sl, off):
            v = xs[sl, :]
            w = alpha * v - beta * (dinv_ref[sl, :] * off)
            store_ext(ext_w, b, w)
            r = res_ref[sl, :]
            if te:
                res_ref[sl, :] = r - alpha * (diag_ref[sl, :] * v) + gamma * off
                sol_ref[sl, :] += w
            else:
                res_ref[sl, :] = gamma * off - alpha * r
                sol_ref[sl, :] += v + w

        local_apply(ext_v, first)

        def second(b, sl, off):
            r = res_ref[sl, :] - off
            res_ref[sl, :] = r
            v = dinv_ref[sl, :] * r
            xs[sl, :] = v
            store_ext(ext_v, b, v)

        local_apply(ext_w, second)
        mid_product(True)
        arrive(ex, True)
        off_below, off_above = ghost_terms(ex)
        dw_below = -beta * (dinv_ref[below_rows, :] * off_below)
        dw_above = -beta * (dinv_ref[above_rows, :] * off_above)
        seen_below = jnp.concatenate([split_lanes(far[ex, 0]), split_lanes(send[ex, 1, :ghost])], axis=0)
        seen_above = jnp.concatenate([split_lanes(send[ex, 0, :ghost]), split_lanes(far[ex, 1])], axis=0)
        next_below = recv[ex, 0, ghost:] - beta * quads(dot(r2[0], seen_below), ghost, width)
        next_above = recv[ex, 1, ghost:] - beta * quads(dot(r2[1], seen_above), ghost, width)
        add_below = jnp.concatenate([split_lanes(next_below), split_lanes(dw_below)], axis=0)
        add_above = jnp.concatenate([split_lanes(dw_above), split_lanes(next_above)], axis=0)
        more_below = quads(dot(a2[: 2 * block, :block], add_below), block, width)
        more_above = quads(dot(a2[last_tile:, block:], add_above), block, width)
        zero = jnp.zeros((ghost, width), f32)
        dr_below = jnp.concatenate([gamma * off_below, zero], axis=0) - more_below
        dr_above = jnp.concatenate([zero, gamma * off_above], axis=0) - more_above
        sol_ref[below_rows, :] += dw_below
        sol_ref[above_rows, :] += dw_above
        for b, dr in ((0, dr_below), (blocks - 1, dr_above)):
            sl = slice(b * block, (b + 1) * block)
            r = res_ref[sl, :] + dr
            res_ref[sl, :] = r
            v = dinv_ref[sl, :] * r
            xs[sl, :] = v
            ext_v[ghost + b * block : ghost + (b + 1) * block, :] = split_lanes(v)

    def restricted(ex):
        depart(ex, False, 0.0, 0.0)

        def restrict(b, sl, off):
            s2[sl, :] = split_lanes((1.0 - OMEGA) * res_ref[sl, :] - OMEGA * off)

        local_apply(ext_v, restrict)
        both = dot(oht_ref[...], s2[...])
        arrive(ex, False)
        off_below, off_above = ghost_terms(ex)
        nothing = jnp.zeros((ghost, 2 * width), bf16)
        ds_below = jnp.concatenate([split_lanes(-OMEGA * off_below), nothing], axis=0)
        ds_above = jnp.concatenate([nothing, split_lanes(-OMEGA * off_above)], axis=0)
        both = both + dot(oht_ref[:, :block], ds_below) + dot(oht_ref[:, rows_dev - block :], ds_above)
        return both[:, :width] + both[:, width:]

    def polynomial():
        half = parts // 2
        eye = iota((agg, agg), 0) == iota((agg, agg), 1)
        cinv = []
        for j in range(parts):
            sl = slice(j * agg, (j + 1) * agg)
            cinv.append(1.0 / jnp.sum(jnp.where(eye, slabs[sl, :agg], 0.0), axis=0, keepdims=True))
            for k in range(half + 1):
                other = (j + k) % parts
                so = slice(other * agg, (other + 1) * agg)
                tile = slabs[sl, k * agg : (k + 1) * agg]
                m_hi[sl, so], m_lo[sl, so] = split(tile)
                if 0 < k and 2 * k < parts:
                    m_hi[so, sl], m_lo[so, sl] = split(tile.T)
        for j in range(parts):
            sl = slice(j * agg, (j + 1) * agg)
            start = jnp.where(jnp.logical_and(eye, me == j), cinv[j], 0.0)
            pd[:, sl] = start
            pz[:, sl] = start
            px[:, sl] = start
        rho_old = RHO0
        for turn in range(1, CHEB_COARSE):
            rho_new = 1.0 / (2.0 * THETA / DELTA - rho_old)
            hi, lo = split(pd[...])
            pair2[:agg, :] = hi
            pair2[agg:, :] = lo
            for j in range(parts // 2):
                sl = slice(2 * j * agg, (2 * j + 2) * agg)
                both = dot(pair2[...], m_hi[:, sl])
                low = dot(pair2[:agg, :], m_lo[:, sl])
                scale = jnp.concatenate([cinv[2 * j], cinv[2 * j + 1]], axis=1)
                z = pz[:, sl] - (both[:agg] + (both[agg:] + low)) * scale
                d = rho_new * rho_old * pd[:, sl] + (2.0 * rho_new / DELTA) * z
                pz[:, sl] = z
                pd[:, sl] = d
                px[:, sl] += d
            rho_old = rho_new
        hi, lo = split(px[...])
        m2[:agg, :] = hi
        m2[agg:, :] = lo

    def gather(step):
        half = n_sub // 2

        def block_copy(source, origin, slot, peer):
            return pltpu.make_async_remote_copy(
                src_ref=source, dst_ref=whole.at[step, aligned(origin * agg, agg)],
                send_sem=csend_sem.at[step, slot], recv_sem=crecv_sem.at[step, slot],
                device_id=(grp, peer), device_id_type=MESH,
            )

        copies = [block_copy(csend.at[step], me, 0, partner)]
        for j in range(1, half):
            copies.append(block_copy(csend.at[step], me, j, lax.rem(me + 2 * j, n_sub)))
        for copy in copies:
            copy.start()
        whole[step, mine, :] = csend[step]
        passed = []
        for j in range(1, half):
            copies[j].wait_recv()
            origin = lax.rem(me + n_sub - 2 * j, n_sub)
            copy = block_copy(whole.at[step, aligned(origin * agg, agg)], origin, half + j, partner)
            copy.start()
            passed.append(copy)
        copies[0].wait_recv()
        for copy in passed:
            copy.wait_recv()
        for copy in copies + passed:
            copy.wait_send()

    for way, d in ((0, 1), (1, -1)):
        @pl.when(has[d])
        def _():
            r_copy(way).start()
    mid_product(True)

    def cycle_body(cycle, carry):
        ex = cycle * ROUNDS

        @pl.when(cycle == 0)
        def _():
            for way, d in ((0, 1), (1, -1)):
                @pl.when(has[-d])
                def _():
                    r_copy(way).wait_recv()

                @pl.when(has[d])
                def _():
                    r_copy(way).wait_send()

                hi, lo = split(r_recv[way])
                r2[way, :ghost] = hi
                r2[way, ghost:] = lo

        pair(ex, False)
        csend[cycle] = restricted(ex + 1)

        @pl.when(cycle == 0)
        def _():
            def rest(event, c):
                slab_pass(event)
                return c

            lax.fori_loop(in_setup, events, rest, 0)
            slab_close()
            polynomial()

        gather(cycle)
        corr = split_lanes(quads(dot(m2[...], split_lanes(whole[cycle])), agg, width))

        def spread(b, c):
            sl = aligned(b * block, block)
            both = dot(oh_ref[sl, :], corr)
            t = both[:, :width] + both[:, width:]
            xs[sl, :] = t
            store_ext(ext_v, b, t)
            return c

        lax.fori_loop(0, blocks, spread, 0, unroll=4)
        mid_product(True)
        pair(ex + 2, True)
        pair(ex + 3, False)
        return carry

    lax.fori_loop(0, CYCLES, cycle_body, 0)


def body(n_grp, n_sub, right_side, fine_values, columns, agg_map, send_lo, send_hi, coarse_matrix):
    rows, width = right_side.shape
    ghost = send_lo.shape[0]
    block = 2 * ghost
    own = coarse_matrix[0]
    agg, coarse = own.shape
    kept = (coarse // agg // 2 + 1) * agg
    ext_rows = rows + block
    exchanges = CYCLES * ROUNDS
    vmem = pl.BlockSpec(memory_space=pltpu.VMEM)
    field = jax.ShapeDtypeStruct((rows, width), f32)
    dma = pltpu.SemaphoreType.DMA
    return pl.pallas_call(
        functools.partial(kernel, n_grp, n_sub),
        in_specs=[vmem] * 7,
        out_specs=[vmem] * 2,
        out_shape=[field] * 2,
        scratch_shapes=[
            pltpu.VMEM((2 * rows, 2 * block), bf16),
            pltpu.VMEM((rows, block), f32),
            pltpu.VMEM((rows, block), f32),
            pltpu.VMEM((rows, agg), bf16),
            pltpu.VMEM((agg, rows), bf16),
            pltpu.VMEM((6 * ghost, ext_rows), bf16),
            pltpu.VMEM((2 * ghost, ext_rows), f32),
            pltpu.VMEM((2 * ghost, block), f32),
            pltpu.VMEM((rows, width), f32),
            pltpu.VMEM((ext_rows, 2 * width), bf16),
            pltpu.VMEM((ext_rows, 2 * width), bf16),
            pltpu.VMEM((rows, 2 * width), bf16),
            pltpu.VMEM((6 * ghost, 2 * width), f32),
            pltpu.VMEM((exchanges, 2, 2 * ghost, width), f32),
            pltpu.VMEM((exchanges, 2, 2 * ghost, width), f32),
            pltpu.VMEM((exchanges, 2, ghost, width), f32),
            pltpu.VMEM((2, ghost, 2 * ghost), f32),
            pltpu.VMEM((2, ghost, 2 * ghost), f32),
            pltpu.VMEM((2, 2 * ghost, 2 * ghost), bf16),
            dma((exchanges, 2)),
            dma((exchanges, 2)),
            dma((exchanges, 2)),
            dma((exchanges, 2)),
            dma((2,)),
            dma((2,)),
            pltpu.VMEM((coarse, kept), f32),
            dma((3, n_sub // 2, CHUNKS)),
            dma((3, n_sub // 2, CHUNKS)),
            pltpu.VMEM((coarse, coarse), bf16),
            pltpu.VMEM((coarse, coarse), bf16),
            pltpu.VMEM((agg, coarse), f32),
            pltpu.VMEM((agg, coarse), f32),
            pltpu.VMEM((agg, coarse), f32),
            pltpu.VMEM((2 * agg, coarse), bf16),
            pltpu.VMEM((2 * agg, coarse), bf16),
            pltpu.VMEM((CYCLES, agg, width), f32),
            pltpu.VMEM((CYCLES, coarse, width), f32),
            dma((CYCLES, n_sub)),
            dma((CYCLES, n_sub)),
        ],
        compiler_params=pltpu.CompilerParams(
            collective_id=0, has_side_effects=True, vmem_limit_bytes=60 * 1024 * 1024
        ),
        name="cycles",
    )(
        right_side, fine_values, columns, agg_map.reshape(1, rows),
        send_lo.reshape(1, ghost), send_hi.reshape(1, ghost), own,
    )


def solution(mesh):
    placed = (
        P(("grp", "sub"), None),
        P(None, ("grp", "sub")),
        P(None, ("grp", "sub")),
        P(("grp", "sub")),
        P(("grp", "sub")),
        P(("grp", "sub")),
        P("grp", "sub", None),
    )
    return jax.shard_map(
        functools.partial(body, mesh.shape["grp"], mesh.shape["sub"]),
        mesh=mesh,
        in_specs=placed,
        out_specs=(P(("grp", "sub"), None), P(("grp", "sub"), None)),
        check_vma=False,
    )
```

```python
import functools

import jax
import jax.numpy as jnp
from jax import lax
from jax.experimental import pallas as pl
from jax.experimental.pallas import tpu as pltpu
from jax.sharding import PartitionSpec as P

CHEB_COARSE = 6
CYCLES = 2
ROUNDS = 4
FIRST = 1
CHUNKS = 4
PIECES = 2

THETA = 1.0
DELTA = 0.7
OMEGA = 0.6
RHO0 = DELTA / THETA
RHO1 = 1.0 / (2.0 * THETA / DELTA - RHO0)
C1 = RHO1 * RHO0
C2 = 2.0 * RHO1 / DELTA
MESH = pl.DeviceIdType.MESH
f32 = jnp.float32
bf16 = jnp.bfloat16


def split(x):
    hi = x.astype(bf16)
    lo = (x - hi.astype(f32)).astype(bf16)
    return hi, lo


def split_lanes(x):
    hi, lo = split(x)
    return jnp.concatenate([hi, lo], axis=1)


def iota(shape, dim):
    return lax.broadcasted_iota(jnp.int32, shape, dim)


def dot(a, b):
    return jnp.dot(a, b, preferred_element_type=f32)


def quads(product, rows, width):
    return product[:rows, :width] + (product[:rows, width:] + product[rows:, :width])


def aligned(start, size):
    return pl.ds(pl.multiple_of(start, size), size)


def band_tile(fv_ref, col_ref, b, block):
    groups = (fv_ref.shape[0] - 1) // 8
    sl = aligned(b * block, block)
    rows = iota((8, block), 1) + b * block
    cols, vals, firsts = [], [], []
    for i in range(groups):
        cols.append(col_ref[1 + 8 * i : 9 + 8 * i, sl] - rows)
        vals.append(fv_ref[1 + 8 * i : 9 + 8 * i, sl])
    last = jnp.zeros((8, block), f32)
    for i in range(groups):
        last = last + jnp.where(cols[i] == block, vals[i], 0.0)
    last = jnp.sum(last, axis=0, keepdims=True)
    for j in range(groups):
        total = vals[j]
        for i in range(j + 1, groups):
            total = total + jnp.where(cols[i] == cols[j], vals[i], 0.0)
        firsts.append(total)
    high_count = block // 8
    places = [iota((8, block), 0) + 8 * h for h in range(high_count)]
    sums = [jnp.zeros((8, block), f32)] * high_count
    for s in range(8):
        chains = [jnp.zeros((8, block), f32)] * high_count
        for i in reversed(range(groups)):
            col = jnp.broadcast_to(cols[i][s : s + 1, :], (8, block))
            val = jnp.broadcast_to(firsts[i][s : s + 1, :], (8, block))
            chains = [jnp.where(col == places[h], val, chains[h]) for h in range(high_count)]
        sums = [sums[h] + chains[h] for h in range(high_count)]
    by_offset = jnp.concatenate(sums, axis=0).T
    skewed = pltpu.roll(by_offset, 0, 1, stride=1, stride_axis=0)
    lane = iota((block, block), 1)
    sub = iota((block, block), 0)
    low = jnp.where(lane >= sub, skewed, 0.0)
    high = jnp.where(lane < sub, skewed, jnp.where(lane == sub, last, 0.0))
    return low, high


def kernel(n_grp, n_sub, *refs):
    ins = refs[:7]
    (sol_ref, res_ref,
     rhs_ref, fv_ref, col_ref, agg_ref, lo_ref, hi_ref, own_ref, in_sem,
     a2, dinv_ref, diag_ref, oh_ref, oht_ref, g_ref, sa, dinv_s,
     xs, ext_v, ext_w, s2, y_mid,
     send, recv, far, r_send, r_recv, r2,
     send_sem, recv_sem, far_send_sem, far_recv_sem, r_send_sem, r_recv_sem,
     slabs, slab_send_sem, slab_recv_sem, cinv_ref, m_hi, m_lo, pd, pz, px, pair2, m2,
     whole, line_send, line_recv, over_send, over_recv, go_ref) = refs[7:]
    held = (rhs_ref, fv_ref, col_ref, agg_ref, lo_ref, hi_ref, own_ref)
    loads = [pltpu.make_async_copy(ins[i], held[i], in_sem.at[i]) for i in range(7)]
    for i in (6, 1, 2, 4, 5, 0, 3):
        loads[i].start()
    rows_dev, width = rhs_ref.shape
    ghost = lo_ref.shape[1]
    block = 2 * ghost
    blocks = rows_dev // block
    agg, coarse = own_ref.shape
    parts = coarse // agg
    kept = slabs.shape[1]
    grp = lax.axis_index("grp")
    me = lax.axis_index("sub")
    total = n_grp * n_sub
    part = grp * n_sub + me
    ones = functools.partial(jnp.asarray, dtype=jnp.int32)

    def device(p):
        return lax.div(p, n_sub), lax.rem(p, n_sub)

    has = {d: jnp.logical_and(part + d >= 0, part + d < total) for d in (1, -1, 2, -2)}

    barrier = pltpu.get_barrier_semaphore()
    for j in range(1, n_sub):
        pl.semaphore_signal(barrier, inc=1, device_id=(grp, lax.rem(me + j, n_sub)), device_id_type=MESH)
    greeted = n_sub - 1
    for d in (1, -1, 2, -2):
        outside = jnp.logical_or(me + d < 0, me + d >= n_sub)
        across = jnp.logical_and(has[d], outside)

        @pl.when(across)
        def _():
            pl.semaphore_signal(barrier, inc=1, device_id=device(part + d), device_id_type=MESH)

        greeted = greeted + across.astype(jnp.int32)

    mine = aligned(me * agg, agg)
    loads[6].wait()
    for k in range(kept // agg):
        slabs[mine, k * agg : (k + 1) * agg] = own_ref[:, aligned(lax.rem(me + k, n_sub) * agg, agg)]
    pl.semaphore_wait(barrier, greeted)

    line = n_sub // 2
    odd = lax.rem(me, 2)
    partner = me + 1 - 2 * odd
    place = jnp.where(odd == 1, lax.div(me, 2), n_sub - 1 - lax.div(me, 2))
    chunk = agg // CHUNKS
    halved = CHUNKS // 2
    UP, DOWN = range(2)

    def at_place(q):
        q = lax.rem(q + n_sub, n_sub)
        return jnp.where(q < line, 2 * q + 1, 2 * (n_sub - 1 - q))

    def origin_of(step, way):
        return at_place(place - step if way == UP else place + step)

    def slab(origin, step, c, way, act):
        peer = at_place(place + 1 if way == UP else place - 1)

        def copy(columns):
            at = pl.ds(pl.multiple_of(origin * agg + c * chunk, chunk), chunk)
            act(pltpu.make_async_remote_copy(
                src_ref=slabs.at[at, pl.ds(0, columns)], dst_ref=slabs.at[at, pl.ds(0, columns)],
                send_sem=slab_send_sem.at[way, step, c], recv_sem=slab_recv_sem.at[way, step, c],
                device_id=(grp, peer), device_id_type=MESH,
            ))

        @pl.when(origin < line)
        def _():
            copy(kept)

        @pl.when(origin >= line)
        def _():
            copy(kept - agg)

    def start(copy):
        copy.start()

    def wait_send(copy):
        copy.wait_send()

    def wait_recv(copy):
        copy.wait_recv()

    def slab_open():
        def one(c, carry):
            for way in (UP, DOWN):
                slab(me, 0, c, way, start)
            return carry

        lax.fori_loop(0, CHUNKS, one, 0)

    events = (line - 1) * CHUNKS + halved

    def slab_passes(first, last):
        def one(event, carry):
            step = lax.div(event, CHUNKS)
            c = lax.rem(event, CHUNKS)
            for way in (UP, DOWN):
                at = c if way == UP else lax.rem(c + halved, CHUNKS)
                origin = origin_of(step + 1, way)
                slab(origin, step, at, way, wait_recv)

                @pl.when(event + CHUNKS < (line - 1) * CHUNKS + halved)
                def _():
                    slab(origin, step + 1, at, way, start)

            return carry

        lax.fori_loop(first, last, one, 0)

    def slab_close():
        def one(event, carry):
            step = lax.div(event, CHUNKS)
            c = lax.rem(event, CHUNKS)
            for way in (UP, DOWN):
                slab(origin_of(step, way), step, c if way == UP else lax.rem(c + halved, CHUNKS), way, wait_send)
            return carry

        lax.fori_loop(0, events, one, 0)

    half = parts // 2
    eye = iota((agg, agg), 0) == iota((agg, agg), 1)

    def take_slab(j):
        sl = aligned(j * agg, agg)
        cinv_ref[:, sl] = 1.0 / jnp.sum(jnp.where(eye, slabs[sl, :agg], 0.0), axis=0, keepdims=True)

        def place_tile(k):
            so = aligned(lax.rem(j + k, parts) * agg, agg)
            tile = slabs[sl, k * agg : (k + 1) * agg]
            m_hi[sl, so], m_lo[sl, so] = split(tile)
            if k:
                m_hi[so, sl], m_lo[so, sl] = split(tile.T)

        for k in range(half):
            place_tile(k)

        @pl.when(j < half)
        def _():
            place_tile(half)

    def take_slabs(first, last):
        def one(step, carry):
            take_slab(origin_of(step, UP))

            @pl.when(jnp.logical_and(step > 0, step < line))
            def _():
                take_slab(origin_of(step, DOWN))

            return carry

        lax.fori_loop(first, last, one, 0)

    slab_open()

    for d, slot in ((-1, 0), (1, 1)):
        @pl.when(jnp.logical_not(has[d]))
        def _():
            recv[:, slot] = jnp.zeros((recv.shape[0],) + recv.shape[2:], f32)
            r_recv[slot] = jnp.zeros(r_recv.shape[1:], f32)

    for d, slot in ((-2, 0), (2, 1)):
        @pl.when(jnp.logical_not(has[d]))
        def _():
            far[:, slot] = jnp.zeros((far.shape[0],) + far.shape[2:], f32)

    for ext in (ext_v, ext_w):
        ext[:ghost, :] = jnp.zeros((ghost, 2 * width), bf16)
        ext[ghost + rows_dev :, :] = jnp.zeros((ghost, 2 * width), bf16)
    for i in (1, 2, 4, 5, 0, 3):
        loads[i].wait()
    sent_row = jnp.concatenate([hi_ref[...], lo_ref[...]], axis=1).astype(f32)
    sent = jnp.broadcast_to(sent_row, (2 * ghost, 2 * ghost)).T.astype(jnp.int32)
    lane = iota((2 * ghost, block), 1)
    for j in range(blocks + 1):
        g_ref[: 2 * ghost, j * block : (j + 1) * block] = (sent + (ghost - j * block) == lane).astype(f32).astype(bf16)
    dinv_s[...] = jnp.zeros_like(dinv_s)
    oh_ref[:ghost, :] = jnp.zeros((ghost, agg), bf16)
    oh_ref[ghost + rows_dev :, :] = jnp.zeros((ghost, agg), bf16)
    sa[:, :block] = jnp.zeros((2 * ghost, block), f32)

    def fine(b):
        sl = aligned(b * block, block)
        low, high = band_tile(fv_ref, col_ref, b, block)
        diag = jnp.broadcast_to(fv_ref[0:1, sl], (block, block)).T
        dinv = 1.0 / diag
        diag_ref[sl, :] = diag
        dinv_ref[sl, :] = dinv
        for at, tile in ((0, low), (block, high)):
            hi, lo = split(tile)
            a2[aligned(b * 2 * block, block), at : at + block] = hi
            a2[aligned(b * 2 * block + block, block), at : at + block] = lo
        rhs = rhs_ref[sl, :]
        res_ref[sl, :] = rhs
        sol_ref[sl, :] = jnp.zeros_like(rhs)
        v = dinv * rhs
        xs[sl, :] = v
        ext_v[pl.ds(pl.multiple_of(ghost + b * block, ghost), block), :] = split_lanes(v)

    def setup(i, carry):
        for u in range(2):
            fine(2 * i + u)
        slab_passes(jnp.clip(i - FIRST, 0, events), jnp.clip(i + 1 - FIRST, 0, events))
        return carry

    lax.fori_loop(0, blocks // 2, setup, 0)
    done = min(blocks // 2 - FIRST, events)
    ends = [done] + [min(done + n, events) for n in (2, 3, 4, 5)]

    def sent_rows(b, carry):
        sl = aligned(b * block, block)
        onehot = (iota((agg, block), 0) == agg_ref[:, sl]).astype(f32)
        oht_ref[:, sl] = onehot.astype(bf16)
        oh_ref[pl.ds(pl.multiple_of(ghost + b * block, ghost), block), :] = onehot.T.astype(bf16)
        picked = (sent - b * block == lane).astype(f32).astype(bf16)
        both = dot(picked, a2[aligned(b * 2 * block, block), :]) + dot(picked, a2[aligned(b * 2 * block + block, block), :])
        sa[:, sl] = sa[:, sl] + both[:, :block]
        sa[:, aligned((b + 1) * block, block)] = both[:, block:]
        both = dot(picked, split_lanes(dinv_ref[sl, :]))
        dinv_s[...] += both[:, :block] + both[:, block:]
        return carry

    lax.fori_loop(0, blocks, sent_rows, 0, unroll=4)
    slab_passes(ends[0], ends[1])
    for j in range(blocks + 1):
        at = slice(j * block, (j + 1) * block)
        scaled = sa[:, at] * dinv_s[...]
        g_ref[2 * ghost : 4 * ghost, at], g_ref[4 * ghost :, at] = split(scaled)
        if j == 0:
            below = scaled
    spread_sent = dot(g_ref[...], oh_ref[...])
    go_ref[: 2 * ghost] = spread_sent[: 2 * ghost].astype(bf16)
    go_ref[2 * ghost : 4 * ghost], go_ref[4 * ghost :] = split(spread_sent[2 * ghost : 4 * ghost] + spread_sent[4 * ghost :])
    response = jnp.where(lane < ghost, below, scaled)
    r_send[0] = response[:ghost]
    r_send[1] = response[ghost:]

    def r_copy(way):
        d = (1, -1)[way]
        return pltpu.make_async_remote_copy(
            src_ref=r_send.at[way], dst_ref=r_recv.at[way],
            send_sem=r_send_sem.at[way], recv_sem=r_recv_sem.at[way],
            device_id=device(part + d), device_id_type=MESH,
        )

    def near_copy(ex, way, count):
        d = (1, -1)[way]
        return pltpu.make_async_remote_copy(
            src_ref=send.at[ex, way, pl.ds(0, count)], dst_ref=recv.at[ex, way, pl.ds(0, count)],
            send_sem=send_sem.at[ex, way], recv_sem=recv_sem.at[ex, way],
            device_id=device(part + d), device_id_type=MESH,
        )

    def far_copy(ex, way):
        d = (2, -2)[way]
        return pltpu.make_async_remote_copy(
            src_ref=send.at[ex, way, pl.ds(0, ghost)], dst_ref=far.at[ex, way],
            send_sem=far_send_sem.at[ex, way], recv_sem=far_recv_sem.at[ex, way],
            device_id=device(part + d), device_id_type=MESH,
        )

    def mid_product(double):
        high = 6 * ghost if double else 2 * ghost
        inner = slice(2 * block, (blocks - 1) * block)
        y_mid[:high] = dot(g_ref[:high, inner], ext_v[inner, :])

    def all_sent(double):
        high = 6 * ghost if double else 2 * ghost
        y = y_mid[:high]
        for rim in (slice(0, 2 * block), slice((blocks - 1) * block, (blocks + 1) * block)):
            y = y + dot(g_ref[:high, rim], ext_v[rim, :])
        return y

    def depart(ex, double, alpha, beta, y):
        now = y[: 2 * ghost, :width] + y[: 2 * ghost, width:]
        for way in range(2):
            send[ex, way, :ghost] = now[way * ghost : (way + 1) * ghost]
        if double:
            later = alpha * now - beta * quads(y[2 * ghost :], 2 * ghost, width)
            for way in range(2):
                send[ex, way, ghost:] = later[way * ghost : (way + 1) * ghost]
        for way, d in ((0, 1), (1, -1)):
            @pl.when(has[d])
            def _():
                near_copy(ex, way, 2 * ghost if double else ghost).start()
        if double:
            for way, d in ((0, 2), (1, -2)):
                @pl.when(has[d])
                def _():
                    far_copy(ex, way).start()

    def arrive(ex, double):
        count = 2 * ghost if double else ghost
        for way, d in ((0, 1), (1, -1)):
            @pl.when(has[-d])
            def _():
                near_copy(ex, way, count).wait_recv()

            @pl.when(has[d])
            def _():
                near_copy(ex, way, count).wait_send()
        if double:
            for way, d in ((0, 2), (1, -2)):
                @pl.when(has[-d])
                def _():
                    far_copy(ex, way).wait_recv()

                @pl.when(has[d])
                def _():
                    far_copy(ex, way).wait_send()

    def local_apply(ext, fn):
        def go(b, carry):
            a = a2[aligned(b * 2 * block, 2 * block), :]
            x = ext[pl.ds(pl.multiple_of(b * block, block), 2 * block), :]
            fn(b, aligned(b * block, block), quads(dot(a, x), block, width))
            return carry

        lax.fori_loop(0, blocks, go, 0, unroll=4)

    def store_ext(ext, b, x):
        ext[pl.ds(pl.multiple_of(ghost + b * block, ghost), block), :] = split_lanes(x)

    last_tile = (blocks - 1) * 2 * block
    below_rows = slice(0, ghost)
    above_rows = slice(rows_dev - ghost, rows_dev)

    def ghost_terms(ex):
        nothing = jnp.zeros((ghost, 2 * width), bf16)
        a_below = jnp.concatenate([a2[:ghost, :block], a2[block : block + ghost, :block]], axis=0)
        a_above = jnp.concatenate(
            [a2[last_tile + ghost : last_tile + block, block:], a2[last_tile + block + ghost : last_tile + 2 * block, block:]],
            axis=0,
        )
        from_below = jnp.concatenate([split_lanes(recv[ex, 0, :ghost]), nothing], axis=0)
        from_above = jnp.concatenate([nothing, split_lanes(recv[ex, 1, :ghost])], axis=0)
        return quads(dot(a_below, from_below), ghost, width), quads(dot(a_above, from_above), ghost, width)

    def pair(ex, te):
        alpha, beta = (1.0 - OMEGA, OMEGA) if te else (C1, C2)
        gamma = OMEGA if te else C2 - 1.0
        if not te:
            depart(ex, True, alpha, beta, all_sent(True))

        def first(b, sl, off):
            v = xs[sl, :]
            w = alpha * v - beta * (dinv_ref[sl, :] * off)
            store_ext(ext_w, b, w)
            r = res_ref[sl, :]
            if te:
                res_ref[sl, :] = r - alpha * (diag_ref[sl, :] * v) + gamma * off
                sol_ref[sl, :] += w
            else:
                res_ref[sl, :] = gamma * off - alpha * r
                sol_ref[sl, :] += v + w

        local_apply(ext_v, first)
        if not te:
            @pl.when(ex == 0)
            def _():
                slab_passes(ends[1], ends[2])

        def second(b, sl, off):
            r = res_ref[sl, :] - off
            res_ref[sl, :] = r
            v = dinv_ref[sl, :] * r
            xs[sl, :] = v
            store_ext(ext_v, b, v)

        local_apply(ext_w, second)
        mid_product(True)
        if not te:
            @pl.when(ex == 0)
            def _():
                slab_passes(ends[2], ends[3])
                take_slabs(0, min(2, ends[3] // CHUNKS + 1))

        arrive(ex, True)
        off_below, off_above = ghost_terms(ex)
        dw_below = -beta * (dinv_ref[below_rows, :] * off_below)
        dw_above = -beta * (dinv_ref[above_rows, :] * off_above)
        seen_below = jnp.concatenate([split_lanes(far[ex, 0]), split_lanes(send[ex, 1, :ghost])], axis=0)
        seen_above = jnp.concatenate([split_lanes(send[ex, 0, :ghost]), split_lanes(far[ex, 1])], axis=0)
        next_below = recv[ex, 0, ghost:] - beta * quads(dot(r2[0], seen_below), ghost, width)
        next_above = recv[ex, 1, ghost:] - beta * quads(dot(r2[1], seen_above), ghost, width)
        add_below = jnp.concatenate([split_lanes(next_below), split_lanes(dw_below)], axis=0)
        add_above = jnp.concatenate([split_lanes(dw_above), split_lanes(next_above)], axis=0)
        more_below = quads(dot(a2[: 2 * block, :block], add_below), block, width)
        more_above = quads(dot(a2[last_tile:, block:], add_above), block, width)
        zero = jnp.zeros((ghost, width), f32)
        dr_below = jnp.concatenate([gamma * off_below, zero], axis=0) - more_below
        dr_above = jnp.concatenate([zero, gamma * off_above], axis=0) - more_above
        sol_ref[below_rows, :] += dw_below
        sol_ref[above_rows, :] += dw_above
        for b, dr in ((0, dr_below), (blocks - 1, dr_above)):
            sl = slice(b * block, (b + 1) * block)
            r = res_ref[sl, :] + dr
            res_ref[sl, :] = r
            v = dinv_ref[sl, :] * r
            xs[sl, :] = v
            ext_v[ghost + b * block : ghost + (b + 1) * block, :] = split_lanes(v)

    def restricted(ex):
        depart(ex, False, 0.0, 0.0, all_sent(False))

        def restrict(b, sl, off):
            s2[sl, :] = split_lanes((1.0 - OMEGA) * res_ref[sl, :] - OMEGA * off)

        local_apply(ext_v, restrict)
        both = dot(oht_ref[...], s2[...])

        @pl.when(ex == 1)
        def _():
            slab_passes(ends[3], ends[4])
            taken = min(2, ends[3] // CHUNKS + 1)
            take_slabs(taken, max(taken, min(3, ends[4] // CHUNKS + 1)))

        arrive(ex, False)
        off_below, off_above = ghost_terms(ex)
        nothing = jnp.zeros((ghost, 2 * width), bf16)
        ds_below = jnp.concatenate([split_lanes(-OMEGA * off_below), nothing], axis=0)
        ds_above = jnp.concatenate([nothing, split_lanes(-OMEGA * off_above)], axis=0)
        both = both + dot(oht_ref[:, :block], ds_below) + dot(oht_ref[:, rows_dev - block :], ds_above)
        return both[:, :width] + both[:, width:]

    def polynomial():
        cinv = [cinv_ref[:, j * agg : (j + 1) * agg] for j in range(parts)]
        first_rho = 1.0 / (2.0 * THETA / DELTA - RHO0)
        mine_diag = own_ref[:, mine]
        mine_inv = 1.0 / jnp.sum(jnp.where(eye, mine_diag, 0.0), axis=1, keepdims=True)
        for j in range(parts):
            sl = slice(j * agg, (j + 1) * agg)
            begin = jnp.where(jnp.logical_and(eye, me == j), cinv[j], 0.0)
            z = begin - (mine_inv * own_ref[:, sl]) * cinv[j]
            d = first_rho * RHO0 * begin + (2.0 * first_rho / DELTA) * z
            pz[:, sl] = z
            pd[:, sl] = d
            px[:, sl] = begin + d
        rho_old = first_rho
        for turn in range(2, CHEB_COARSE):
            rho_new = 1.0 / (2.0 * THETA / DELTA - rho_old)
            hi, lo = split(pd[...])
            pair2[:agg, :] = hi
            pair2[agg:, :] = lo
            for j in range(parts // 2):
                sl = slice(2 * j * agg, (2 * j + 2) * agg)
                both = dot(pair2[...], m_hi[:, sl])
                low = dot(pair2[:agg, :], m_lo[:, sl])
                scale = jnp.concatenate([cinv[2 * j], cinv[2 * j + 1]], axis=1)
                z = pz[:, sl] - (both[:agg] + (both[agg:] + low)) * scale
                d = rho_new * rho_old * pd[:, sl] + (2.0 * rho_new / DELTA) * z
                pz[:, sl] = z
                pd[:, sl] = d
                px[:, sl] += d
            rho_old = rho_new
        hi, lo = split(px[...])
        m2[:agg, :] = hi
        m2[agg:, :] = lo

    pos = lax.div(me, 2)
    part_rows = agg // PIECES

    def coarse_copy(step, origin, c, peer, sends, recvs):
        at = pl.ds(pl.multiple_of(origin * agg + c * part_rows, part_rows), part_rows)
        return pltpu.make_async_remote_copy(
            src_ref=whole.at[step, at], dst_ref=whole.at[step, at], send_sem=sends, recv_sem=recvs,
            device_id=(grp, peer), device_id_type=MESH,
        )

    def along(step, far_by, way, c, origin):
        peer = me + 2 * far_by if way == UP else me - 2 * far_by
        return coarse_copy(step, origin, c, peer, line_send.at[step, way, far_by - 1, c], line_recv.at[step, way, far_by - 1, c])

    def over(step, c, origin):
        q = lax.div(origin, 2)
        return coarse_copy(step, origin, c, partner, over_send.at[step, q, c], over_recv.at[step, q, c])

    def reaches(far_by, way):
        return pos + far_by < line if way == UP else pos - far_by >= 0

    def gather_open(step):
        for c in range(PIECES):
            over(step, c, me).start()
            for far_by in reversed(range(1, line)):
                for way in (UP, DOWN):
                    @pl.when(reaches(far_by, way))
                    def _():
                        along(step, far_by, way, c, me).start()

    def gather_pass(step):
        for far_by in range(1, line):
            for c in range(PIECES):
                for way in (UP, DOWN):
                    @pl.when(reaches(far_by, 1 - way))
                    def _():
                        origin = me - 2 * far_by if way == UP else me + 2 * far_by
                        along(step, far_by, way, c, origin).wait_recv()
                        over(step, c, origin).start()

    def gather_close(step):
        for c in range(PIECES):
            for q in range(line):
                over(step, c, 2 * q + 1 - odd).wait_recv()
                over(step, c, 2 * q + odd).wait_send()
            for far_by in range(1, line):
                for way in (UP, DOWN):
                    @pl.when(reaches(far_by, way))
                    def _():
                        along(step, far_by, way, c, me).wait_send()

    for way, d in ((0, 1), (1, -1)):
        @pl.when(has[d])
        def _():
            r_copy(way).start()
    mid_product(True)

    def cycle_body(cycle, carry):
        ex = cycle * ROUNDS

        @pl.when(cycle == 0)
        def _():
            for way, d in ((0, 1), (1, -1)):
                @pl.when(has[-d])
                def _():
                    r_copy(way).wait_recv()

                @pl.when(has[d])
                def _():
                    r_copy(way).wait_send()

                hi, lo = split(r_recv[way])
                r2[way, :ghost] = hi
                r2[way, ghost:] = lo

        pair(ex, False)
        whole[cycle, mine, :] = restricted(ex + 1)
        gather_open(cycle)

        @pl.when(cycle == 0)
        def _():
            slab_passes(ends[4], events)

        gather_pass(cycle)

        @pl.when(cycle == 0)
        def _():
            slab_close()
            take_slabs(max(min(2, ends[3] // CHUNKS + 1), min(3, ends[4] // CHUNKS + 1)), line + 1)
            polynomial()

        gather_close(cycle)
        corr = split_lanes(quads(dot(m2[...], split_lanes(whole[cycle])), agg, width))
        depart(ex + 2, True, 1.0 - OMEGA, OMEGA, dot(go_ref[...], corr))

        def spread(b, c):
            sl = aligned(b * block, block)
            both = dot(oh_ref[pl.ds(pl.multiple_of(ghost + b * block, ghost), block), :], corr)
            t = both[:, :width] + both[:, width:]
            xs[sl, :] = t
            store_ext(ext_v, b, t)
            return c

        lax.fori_loop(0, blocks, spread, 0, unroll=4)
        pair(ex + 2, True)
        pair(ex + 3, False)
        return carry

    lax.fori_loop(0, CYCLES, cycle_body, 0)


def store_kernel(a_ref, b_ref, c_ref, d_ref, sem):
    copies = [pltpu.make_async_copy(a_ref, c_ref, sem.at[0]), pltpu.make_async_copy(b_ref, d_ref, sem.at[1])]
    for copy in copies:
        copy.start()
    for copy in copies:
        copy.wait()


def store(sol, res):
    return pl.pallas_call(
        store_kernel,
        in_specs=[pl.BlockSpec(memory_space=pltpu.VMEM)] * 2,
        out_specs=[pl.BlockSpec(memory_space=pltpu.HBM)] * 2,
        out_shape=[jax.ShapeDtypeStruct(sol.shape, f32)] * 2,
        scratch_shapes=[pltpu.SemaphoreType.DMA((2,))],
        name="store",
    )(sol, res)


def body(n_grp, n_sub, right_side, fine_values, columns, agg_map, send_lo, send_hi, coarse_matrix):
    rows, width = right_side.shape
    ghost = send_lo.shape[0]
    block = 2 * ghost
    own = coarse_matrix[0]
    agg, coarse = own.shape
    kept = (coarse // agg // 2 + 1) * agg
    ext_rows = rows + block
    exchanges = CYCLES * ROUNDS
    vmem = pl.BlockSpec(memory_space=pltpu.VMEM)
    field = jax.ShapeDtypeStruct((rows, width), f32)
    dma = pltpu.SemaphoreType.DMA
    sol, res = pl.pallas_call(
        functools.partial(kernel, n_grp, n_sub),
        in_specs=[pl.BlockSpec(memory_space=pltpu.HBM)] * 7,
        out_specs=[vmem] * 2,
        out_shape=[field] * 2,
        scratch_shapes=[
            pltpu.VMEM((rows, width), f32),
            pltpu.VMEM(fine_values.shape, f32),
            pltpu.VMEM(columns.shape, jnp.int32),
            pltpu.VMEM((1, rows), jnp.int32),
            pltpu.VMEM((1, ghost), jnp.int32),
            pltpu.VMEM((1, ghost), jnp.int32),
            pltpu.VMEM((agg, coarse), f32),
            dma((7,)),
            pltpu.VMEM((2 * rows, 2 * block), bf16),
            pltpu.VMEM((rows, block), f32),
            pltpu.VMEM((rows, block), f32),
            pltpu.VMEM((ext_rows, agg), bf16),
            pltpu.VMEM((agg, rows), bf16),
            pltpu.VMEM((6 * ghost, ext_rows), bf16),
            pltpu.VMEM((2 * ghost, ext_rows), f32),
            pltpu.VMEM((2 * ghost, block), f32),
            pltpu.VMEM((rows, width), f32),
            pltpu.VMEM((ext_rows, 2 * width), bf16),
            pltpu.VMEM((ext_rows, 2 * width), bf16),
            pltpu.VMEM((rows, 2 * width), bf16),
            pltpu.VMEM((6 * ghost, 2 * width), f32),
            pltpu.VMEM((exchanges, 2, 2 * ghost, width), f32),
            pltpu.VMEM((exchanges, 2, 2 * ghost, width), f32),
            pltpu.VMEM((exchanges, 2, ghost, width), f32),
            pltpu.VMEM((2, ghost, 2 * ghost), f32),
            pltpu.VMEM((2, ghost, 2 * ghost), f32),
            pltpu.VMEM((2, 2 * ghost, 2 * ghost), bf16),
            dma((exchanges, 2)),
            dma((exchanges, 2)),
            dma((exchanges, 2)),
            dma((exchanges, 2)),
            dma((2,)),
            dma((2,)),
            pltpu.VMEM((coarse, kept), f32),
            dma((2, n_sub // 2, CHUNKS)),
            dma((2, n_sub // 2, CHUNKS)),
            pltpu.VMEM((1, coarse), f32),
            pltpu.VMEM((coarse, coarse), bf16),
            pltpu.VMEM((coarse, coarse), bf16),
            pltpu.VMEM((agg, coarse), f32),
            pltpu.VMEM((agg, coarse), f32),
            pltpu.VMEM((agg, coarse), f32),
            pltpu.VMEM((2 * agg, coarse), bf16),
            pltpu.VMEM((2 * agg, coarse), bf16),
            pltpu.VMEM((CYCLES, coarse, width), f32),
            dma((CYCLES, 2, n_sub // 2 - 1, PIECES)),
            dma((CYCLES, 2, n_sub // 2 - 1, PIECES)),
            dma((CYCLES, n_sub // 2, PIECES)),
            dma((CYCLES, n_sub // 2, PIECES)),
            pltpu.VMEM((6 * ghost, agg), bf16),
        ],
        compiler_params=pltpu.CompilerParams(
            collective_id=0, has_side_effects=True, vmem_limit_bytes=60 * 1024 * 1024
        ),
        name="cycles",
    )(
        right_side, fine_values, columns, agg_map.reshape(1, rows),
        send_lo.reshape(1, ghost), send_hi.reshape(1, ghost), own,
    )
    return sol, res


def solution(mesh):
    placed = (
        P(("grp", "sub"), None),
        P(None, ("grp", "sub")),
        P(None, ("grp", "sub")),
        P(("grp", "sub")),
        P(("grp", "sub")),
        P(("grp", "sub")),
        P("grp", "sub", None),
    )
    return jax.shard_map(
        functools.partial(body, mesh.shape["grp"], mesh.shape["sub"]),
        mesh=mesh,
        in_specs=placed,
        out_specs=(P(("grp", "sub"), None), P(("grp", "sub"), None)),
        check_vma=False,
    )
```

```python
import functools

import jax
import jax.numpy as jnp
from jax import lax
from jax.experimental import pallas as pl
from jax.experimental.pallas import tpu as pltpu
from jax.sharding import PartitionSpec as P

CHEB_COARSE = 6
CYCLES = 2
ROUNDS = 4
FIRST = 3
CHUNKS = 4
PIECES = 2

THETA = 1.0
DELTA = 0.7
OMEGA = 0.6
RHO0 = DELTA / THETA
RHO1 = 1.0 / (2.0 * THETA / DELTA - RHO0)
C1 = RHO1 * RHO0
C2 = 2.0 * RHO1 / DELTA
MESH = pl.DeviceIdType.MESH
f32 = jnp.float32
bf16 = jnp.bfloat16


def split(x):
    hi = x.astype(bf16)
    lo = (x - hi.astype(f32)).astype(bf16)
    return hi, lo


def split_lanes(x):
    hi, lo = split(x)
    return jnp.concatenate([hi, lo], axis=1)


def iota(shape, dim):
    return lax.broadcasted_iota(jnp.int32, shape, dim)


def dot(a, b):
    return jnp.dot(a, b, preferred_element_type=f32)


def quads(product, rows, width):
    return product[:rows, :width] + (product[:rows, width:] + product[rows:, :width])


def aligned(start, size):
    return pl.ds(pl.multiple_of(start, size), size)


def band_tile(fv_ref, col_ref, b, block):
    groups = (fv_ref.shape[0] - 1) // 8
    sl = aligned(b * block, block)
    rows = iota((8, block), 1) + b * block
    cols, vals, firsts = [], [], []
    for i in range(groups):
        cols.append(col_ref[1 + 8 * i : 9 + 8 * i, sl] - rows)
        vals.append(fv_ref[1 + 8 * i : 9 + 8 * i, sl])
    last = jnp.zeros((8, block), f32)
    for i in range(groups):
        last = last + jnp.where(cols[i] == block, vals[i], 0.0)
    last = jnp.sum(last, axis=0, keepdims=True)
    for j in range(groups):
        total = vals[j]
        for i in range(j + 1, groups):
            total = total + jnp.where(cols[i] == cols[j], vals[i], 0.0)
        firsts.append(total)
    high_count = block // 8
    places = [iota((8, block), 0) + 8 * h for h in range(high_count)]
    sums = [jnp.zeros((8, block), f32)] * high_count
    for s in range(8):
        chains = [jnp.zeros((8, block), f32)] * high_count
        for i in reversed(range(groups)):
            col = jnp.broadcast_to(cols[i][s : s + 1, :], (8, block))
            val = jnp.broadcast_to(firsts[i][s : s + 1, :], (8, block))
            chains = [jnp.where(col == places[h], val, chains[h]) for h in range(high_count)]
        sums = [sums[h] + chains[h] for h in range(high_count)]
    by_offset = jnp.concatenate(sums, axis=0).T
    skewed = pltpu.roll(by_offset, 0, 1, stride=1, stride_axis=0)
    lane = iota((block, block), 1)
    sub = iota((block, block), 0)
    low = jnp.where(lane >= sub, skewed, 0.0)
    high = jnp.where(lane < sub, skewed, jnp.where(lane == sub, last, 0.0))
    return low, high


def kernel(n_grp, n_sub, *refs):
    ins = refs[:7]
    (sol_ref, res_ref,
     rhs_ref, fv_ref, col_ref, agg_ref, lo_ref, hi_ref, own_ref, in_sem,
     a2, dinv_ref, diag_ref, oh_ref, oht_ref, g_ref, sa, dinv_s,
     xs, ext_v, ext_w, s2, y_mid,
     send, recv, far, r_send, r_recv, r2,
     send_sem, recv_sem, far_send_sem, far_recv_sem, r_send_sem, r_recv_sem,
     slabs, slab_send_sem, slab_recv_sem, cinv_ref, m_hi, m_lo, pd, pz, px, pair2, m2,
     whole, line_send, line_recv, over_send, over_recv, go_ref) = refs[7:]
    held = (rhs_ref, fv_ref, col_ref, agg_ref, lo_ref, hi_ref, own_ref)
    loads = [pltpu.make_async_copy(ins[i], held[i], in_sem.at[i]) for i in range(7)]
    for i in (6, 1, 2, 4, 5, 0, 3):
        loads[i].start()
    rows_dev, width = rhs_ref.shape
    ghost = lo_ref.shape[1]
    block = 2 * ghost
    blocks = rows_dev // block
    agg, coarse = own_ref.shape
    parts = coarse // agg
    kept = slabs.shape[1]
    grp = lax.axis_index("grp")
    me = lax.axis_index("sub")
    total = n_grp * n_sub
    part = grp * n_sub + me
    ones = functools.partial(jnp.asarray, dtype=jnp.int32)

    def device(p):
        return lax.div(p, n_sub), lax.rem(p, n_sub)

    has = {d: jnp.logical_and(part + d >= 0, part + d < total) for d in (1, -1, 2, -2)}

    barrier = pltpu.get_barrier_semaphore()
    for j in range(1, n_sub):
        pl.semaphore_signal(barrier, inc=1, device_id=(grp, lax.rem(me + j, n_sub)), device_id_type=MESH)
    greeted = n_sub - 1
    for d in (1, -1, 2, -2):
        outside = jnp.logical_or(me + d < 0, me + d >= n_sub)
        across = jnp.logical_and(has[d], outside)

        @pl.when(across)
        def _():
            pl.semaphore_signal(barrier, inc=1, device_id=device(part + d), device_id_type=MESH)

        greeted = greeted + across.astype(jnp.int32)

    mine = aligned(me * agg, agg)
    loads[6].wait()
    for k in range(kept // agg):
        slabs[mine, k * agg : (k + 1) * agg] = own_ref[:, aligned(lax.rem(me + k, n_sub) * agg, agg)]
    pl.semaphore_wait(barrier, greeted)

    line = n_sub // 2
    odd = lax.rem(me, 2)
    partner = me + 1 - 2 * odd
    place = jnp.where(odd == 1, lax.div(me, 2), n_sub - 1 - lax.div(me, 2))
    chunk = agg // CHUNKS
    halved = CHUNKS // 2
    UP, DOWN = range(2)

    def at_place(q):
        q = lax.rem(q + n_sub, n_sub)
        return jnp.where(q < line, 2 * q + 1, 2 * (n_sub - 1 - q))

    def origin_of(step, way):
        return at_place(place - step if way == UP else place + step)

    def slab(origin, step, c, way, act):
        peer = at_place(place + 1 if way == UP else place - 1)

        def copy(columns):
            at = pl.ds(pl.multiple_of(origin * agg + c * chunk, chunk), chunk)
            act(pltpu.make_async_remote_copy(
                src_ref=slabs.at[at, pl.ds(0, columns)], dst_ref=slabs.at[at, pl.ds(0, columns)],
                send_sem=slab_send_sem.at[way, step, c], recv_sem=slab_recv_sem.at[way, step, c],
                device_id=(grp, peer), device_id_type=MESH,
            ))

        @pl.when(origin < line)
        def _():
            copy(kept)

        @pl.when(origin >= line)
        def _():
            copy(kept - agg)

    def start(copy):
        copy.start()

    def wait_send(copy):
        copy.wait_send()

    def wait_recv(copy):
        copy.wait_recv()

    def slab_open():
        def one(c, carry):
            for way in (UP, DOWN):
                slab(me, 0, c, way, start)
            return carry

        lax.fori_loop(0, CHUNKS, one, 0)

    events = (line - 1) * CHUNKS + halved

    def slab_passes(first, last):
        def one(event, carry):
            step = lax.div(event, CHUNKS)
            c = lax.rem(event, CHUNKS)
            for way in (UP, DOWN):
                at = c if way == UP else lax.rem(c + halved, CHUNKS)
                origin = origin_of(step + 1, way)
                slab(origin, step, at, way, wait_recv)

                @pl.when(event + CHUNKS < (line - 1) * CHUNKS + halved)
                def _():
                    slab(origin, step + 1, at, way, start)

            return carry

        lax.fori_loop(first, last, one, 0)

    def slab_close():
        def one(event, carry):
            step = lax.div(event, CHUNKS)
            c = lax.rem(event, CHUNKS)
            for way in (UP, DOWN):
                slab(origin_of(step, way), step, c if way == UP else lax.rem(c + halved, CHUNKS), way, wait_send)
            return carry

        lax.fori_loop(0, events, one, 0)

    half = parts // 2
    eye = iota((agg, agg), 0) == iota((agg, agg), 1)

    def take_slab(j):
        sl = aligned(j * agg, agg)
        cinv_ref[:, sl] = 1.0 / jnp.sum(jnp.where(eye, slabs[sl, :agg], 0.0), axis=0, keepdims=True)

        def place_tile(k):
            so = aligned(lax.rem(j + k, parts) * agg, agg)
            tile = slabs[sl, k * agg : (k + 1) * agg]
            m_hi[sl, so], m_lo[sl, so] = split(tile)
            if k:
                m_hi[so, sl], m_lo[so, sl] = split(tile.T)

        for k in range(half):
            place_tile(k)

        @pl.when(j < half)
        def _():
            place_tile(half)

    def take_slabs(first, last):
        def one(step, carry):
            take_slab(origin_of(step, UP))

            @pl.when(jnp.logical_and(step > 0, step < line))
            def _():
                take_slab(origin_of(step, DOWN))

            return carry

        lax.fori_loop(first, last, one, 0)

    slab_open()

    for d, slot in ((-1, 0), (1, 1)):
        @pl.when(jnp.logical_not(has[d]))
        def _():
            recv[:, slot] = jnp.zeros((recv.shape[0],) + recv.shape[2:], f32)
            r_recv[slot] = jnp.zeros(r_recv.shape[1:], f32)

    for d, slot in ((-2, 0), (2, 1)):
        @pl.when(jnp.logical_not(has[d]))
        def _():
            far[:, slot] = jnp.zeros((far.shape[0],) + far.shape[2:], f32)

    for ext in (ext_v, ext_w):
        ext[:ghost, :] = jnp.zeros((ghost, 2 * width), bf16)
        ext[ghost + rows_dev :, :] = jnp.zeros((ghost, 2 * width), bf16)
    for i in (1, 2, 4, 5, 0, 3):
        loads[i].wait()
    sent_row = jnp.concatenate([hi_ref[...], lo_ref[...]], axis=1).astype(f32)
    sent = jnp.broadcast_to(sent_row, (2 * ghost, 2 * ghost)).T.astype(jnp.int32)
    lane = iota((2 * ghost, block), 1)
    for j in range(blocks + 1):
        g_ref[: 2 * ghost, j * block : (j + 1) * block] = (sent + (ghost - j * block) == lane).astype(f32).astype(bf16)
    dinv_s[...] = jnp.zeros_like(dinv_s)
    oh_ref[:ghost, :] = jnp.zeros((ghost, agg), bf16)
    oh_ref[ghost + rows_dev :, :] = jnp.zeros((ghost, agg), bf16)
    sa[:, :block] = jnp.zeros((2 * ghost, block), f32)

    def fine(b):
        sl = aligned(b * block, block)
        low, high = band_tile(fv_ref, col_ref, b, block)
        diag = jnp.broadcast_to(fv_ref[0:1, sl], (block, block)).T
        dinv = 1.0 / diag
        diag_ref[sl, :] = diag
        dinv_ref[sl, :] = dinv
        for at, tile in ((0, low), (block, high)):
            hi, lo = split(tile)
            a2[aligned(b * 2 * block, block), at : at + block] = hi
            a2[aligned(b * 2 * block + block, block), at : at + block] = lo
        rhs = rhs_ref[sl, :]
        res_ref[sl, :] = rhs
        sol_ref[sl, :] = jnp.zeros_like(rhs)
        v = dinv * rhs
        xs[sl, :] = v
        ext_v[pl.ds(pl.multiple_of(ghost + b * block, ghost), block), :] = split_lanes(v)

    def setup(i, carry):
        for u in range(2):
            fine(2 * i + u)
        slab_passes(jnp.clip(i - FIRST, 0, events), jnp.clip(i + 1 - FIRST, 0, events))
        return carry

    lax.fori_loop(0, blocks // 2, setup, 0)
    done = min(blocks // 2 - FIRST, events)
    ends = [done] + [min(done + n, events) for n in (0, 2, 3, 5)]

    def sent_rows(b, carry):
        sl = aligned(b * block, block)
        onehot = (iota((agg, block), 0) == agg_ref[:, sl]).astype(f32)
        oht_ref[:, sl] = onehot.astype(bf16)
        oh_ref[pl.ds(pl.multiple_of(ghost + b * block, ghost), block), :] = onehot.T.astype(bf16)
        picked = (sent - b * block == lane).astype(f32).astype(bf16)
        both = dot(picked, a2[aligned(b * 2 * block, block), :]) + dot(picked, a2[aligned(b * 2 * block + block, block), :])
        sa[:, sl] = sa[:, sl] + both[:, :block]
        sa[:, aligned((b + 1) * block, block)] = both[:, block:]
        both = dot(picked, split_lanes(dinv_ref[sl, :]))
        dinv_s[...] += both[:, :block] + both[:, block:]
        return carry

    lax.fori_loop(0, blocks, sent_rows, 0, unroll=4)
    slab_passes(ends[0], ends[1])
    for j in range(blocks + 1):
        at = slice(j * block, (j + 1) * block)
        scaled = sa[:, at] * dinv_s[...]
        g_ref[2 * ghost : 4 * ghost, at], g_ref[4 * ghost :, at] = split(scaled)
        if j == 0:
            below = scaled
    spread_sent = dot(g_ref[...], oh_ref[...])
    go_ref[: 2 * ghost] = spread_sent[: 2 * ghost].astype(bf16)
    go_ref[2 * ghost : 4 * ghost], go_ref[4 * ghost :] = split(spread_sent[2 * ghost : 4 * ghost] + spread_sent[4 * ghost :])
    response = jnp.where(lane < ghost, below, scaled)
    r_send[0] = response[:ghost]
    r_send[1] = response[ghost:]

    def r_copy(way):
        d = (1, -1)[way]
        return pltpu.make_async_remote_copy(
            src_ref=r_send.at[way], dst_ref=r_recv.at[way],
            send_sem=r_send_sem.at[way], recv_sem=r_recv_sem.at[way],
            device_id=device(part + d), device_id_type=MESH,
        )

    def near_copy(ex, way, count):
        d = (1, -1)[way]
        return pltpu.make_async_remote_copy(
            src_ref=send.at[ex, way, pl.ds(0, count)], dst_ref=recv.at[ex, way, pl.ds(0, count)],
            send_sem=send_sem.at[ex, way], recv_sem=recv_sem.at[ex, way],
            device_id=device(part + d), device_id_type=MESH,
        )

    def far_copy(ex, way):
        d = (2, -2)[way]
        return pltpu.make_async_remote_copy(
            src_ref=send.at[ex, way, pl.ds(0, ghost)], dst_ref=far.at[ex, way],
            send_sem=far_send_sem.at[ex, way], recv_sem=far_recv_sem.at[ex, way],
            device_id=device(part + d), device_id_type=MESH,
        )

    def mid_product(double):
        high = 6 * ghost if double else 2 * ghost
        inner = slice(2 * block, (blocks - 1) * block)
        y_mid[:high] = dot(g_ref[:high, inner], ext_v[inner, :])

    def all_sent(double):
        high = 6 * ghost if double else 2 * ghost
        y = y_mid[:high]
        for rim in (slice(0, 2 * block), slice((blocks - 1) * block, (blocks + 1) * block)):
            y = y + dot(g_ref[:high, rim], ext_v[rim, :])
        return y

    def depart(ex, double, alpha, beta, y):
        now = y[: 2 * ghost, :width] + y[: 2 * ghost, width:]
        for way in range(2):
            send[ex, way, :ghost] = now[way * ghost : (way + 1) * ghost]
        if double:
            later = alpha * now - beta * quads(y[2 * ghost :], 2 * ghost, width)
            for way in range(2):
                send[ex, way, ghost:] = later[way * ghost : (way + 1) * ghost]
        for way, d in ((0, 1), (1, -1)):
            @pl.when(has[d])
            def _():
                near_copy(ex, way, 2 * ghost if double else ghost).start()
        if double:
            for way, d in ((0, 2), (1, -2)):
                @pl.when(has[d])
                def _():
                    far_copy(ex, way).start()

    def arrive(ex, double):
        count = 2 * ghost if double else ghost
        for way, d in ((0, 1), (1, -1)):
            @pl.when(has[-d])
            def _():
                near_copy(ex, way, count).wait_recv()

            @pl.when(has[d])
            def _():
                near_copy(ex, way, count).wait_send()
        if double:
            for way, d in ((0, 2), (1, -2)):
                @pl.when(has[-d])
                def _():
                    far_copy(ex, way).wait_recv()

                @pl.when(has[d])
                def _():
                    far_copy(ex, way).wait_send()

    def local_apply(ext, fn):
        def go(b, carry):
            a = a2[aligned(b * 2 * block, 2 * block), :]
            x = ext[pl.ds(pl.multiple_of(b * block, block), 2 * block), :]
            fn(b, aligned(b * block, block), quads(dot(a, x), block, width))
            return carry

        lax.fori_loop(0, blocks, go, 0, unroll=4)

    def store_ext(ext, b, x):
        ext[pl.ds(pl.multiple_of(ghost + b * block, ghost), block), :] = split_lanes(x)

    last_tile = (blocks - 1) * 2 * block
    below_rows = slice(0, ghost)
    above_rows = slice(rows_dev - ghost, rows_dev)

    def ghost_terms(ex):
        nothing = jnp.zeros((ghost, 2 * width), bf16)
        a_below = jnp.concatenate([a2[:ghost, :block], a2[block : block + ghost, :block]], axis=0)
        a_above = jnp.concatenate(
            [a2[last_tile + ghost : last_tile + block, block:], a2[last_tile + block + ghost : last_tile + 2 * block, block:]],
            axis=0,
        )
        from_below = jnp.concatenate([split_lanes(recv[ex, 0, :ghost]), nothing], axis=0)
        from_above = jnp.concatenate([nothing, split_lanes(recv[ex, 1, :ghost])], axis=0)
        return quads(dot(a_below, from_below), ghost, width), quads(dot(a_above, from_above), ghost, width)

    def pair(ex, te):
        alpha, beta = (1.0 - OMEGA, OMEGA) if te else (C1, C2)
        gamma = OMEGA if te else C2 - 1.0
        if not te:
            depart(ex, True, alpha, beta, all_sent(True))

        def first(b, sl, off):
            v = xs[sl, :]
            w = alpha * v - beta * (dinv_ref[sl, :] * off)
            store_ext(ext_w, b, w)
            r = res_ref[sl, :]
            if te:
                res_ref[sl, :] = r - alpha * (diag_ref[sl, :] * v) + gamma * off
                sol_ref[sl, :] += w
            else:
                res_ref[sl, :] = gamma * off - alpha * r
                sol_ref[sl, :] += v + w

        local_apply(ext_v, first)
        if not te:
            @pl.when(ex == 0)
            def _():
                slab_passes(ends[1], ends[2])

        def second(b, sl, off):
            r = res_ref[sl, :] - off
            res_ref[sl, :] = r
            v = dinv_ref[sl, :] * r
            xs[sl, :] = v
            store_ext(ext_v, b, v)

        local_apply(ext_w, second)
        mid_product(True)
        if not te:
            @pl.when(ex == 0)
            def _():
                slab_passes(ends[2], ends[3])
                take_slabs(0, min(2, ends[3] // CHUNKS + 1))

        arrive(ex, True)
        off_below, off_above = ghost_terms(ex)
        dw_below = -beta * (dinv_ref[below_rows, :] * off_below)
        dw_above = -beta * (dinv_ref[above_rows, :] * off_above)
        seen_below = jnp.concatenate([split_lanes(far[ex, 0]), split_lanes(send[ex, 1, :ghost])], axis=0)
        seen_above = jnp.concatenate([split_lanes(send[ex, 0, :ghost]), split_lanes(far[ex, 1])], axis=0)
        next_below = recv[ex, 0, ghost:] - beta * quads(dot(r2[0], seen_below), ghost, width)
        next_above = recv[ex, 1, ghost:] - beta * quads(dot(r2[1], seen_above), ghost, width)
        add_below = jnp.concatenate([split_lanes(next_below), split_lanes(dw_below)], axis=0)
        add_above = jnp.concatenate([split_lanes(dw_above), split_lanes(next_above)], axis=0)
        more_below = quads(dot(a2[: 2 * block, :block], add_below), block, width)
        more_above = quads(dot(a2[last_tile:, block:], add_above), block, width)
        zero = jnp.zeros((ghost, width), f32)
        dr_below = jnp.concatenate([gamma * off_below, zero], axis=0) - more_below
        dr_above = jnp.concatenate([zero, gamma * off_above], axis=0) - more_above
        sol_ref[below_rows, :] += dw_below
        sol_ref[above_rows, :] += dw_above
        for b, dr in ((0, dr_below), (blocks - 1, dr_above)):
            sl = slice(b * block, (b + 1) * block)
            r = res_ref[sl, :] + dr
            res_ref[sl, :] = r
            v = dinv_ref[sl, :] * r
            xs[sl, :] = v
            ext_v[ghost + b * block : ghost + (b + 1) * block, :] = split_lanes(v)

    def restricted(ex):
        depart(ex, False, 0.0, 0.0, all_sent(False))

        def restrict(b, sl, off):
            s2[sl, :] = split_lanes((1.0 - OMEGA) * res_ref[sl, :] - OMEGA * off)

        local_apply(ext_v, restrict)
        both = dot(oht_ref[...], s2[...])

        @pl.when(ex == 1)
        def _():
            slab_passes(ends[3], ends[4])
            taken = min(2, ends[3] // CHUNKS + 1)
            take_slabs(taken, max(taken, min(3, ends[4] // CHUNKS + 1)))

        arrive(ex, False)
        off_below, off_above = ghost_terms(ex)
        nothing = jnp.zeros((ghost, 2 * width), bf16)
        ds_below = jnp.concatenate([split_lanes(-OMEGA * off_below), nothing], axis=0)
        ds_above = jnp.concatenate([nothing, split_lanes(-OMEGA * off_above)], axis=0)
        both = both + dot(oht_ref[:, :block], ds_below) + dot(oht_ref[:, rows_dev - block :], ds_above)
        return both[:, :width] + both[:, width:]

    def polynomial():
        cinv = [cinv_ref[:, j * agg : (j + 1) * agg] for j in range(parts)]
        first_rho = 1.0 / (2.0 * THETA / DELTA - RHO0)
        mine_diag = own_ref[:, mine]
        mine_inv = 1.0 / jnp.sum(jnp.where(eye, mine_diag, 0.0), axis=1, keepdims=True)
        for j in range(parts):
            sl = slice(j * agg, (j + 1) * agg)
            begin = jnp.where(jnp.logical_and(eye, me == j), cinv[j], 0.0)
            z = begin - (mine_inv * own_ref[:, sl]) * cinv[j]
            d = first_rho * RHO0 * begin + (2.0 * first_rho / DELTA) * z
            pz[:, sl] = z
            pd[:, sl] = d
            px[:, sl] = begin + d
        rho_old = first_rho
        for turn in range(2, CHEB_COARSE):
            rho_new = 1.0 / (2.0 * THETA / DELTA - rho_old)
            hi, lo = split(pd[...])
            pair2[:agg, :] = hi
            pair2[agg:, :] = lo
            for j in range(parts // 2):
                sl = slice(2 * j * agg, (2 * j + 2) * agg)
                both = dot(pair2[...], m_hi[:, sl])
                low = dot(pair2[:agg, :], m_lo[:, sl])
                scale = jnp.concatenate([cinv[2 * j], cinv[2 * j + 1]], axis=1)
                z = pz[:, sl] - (both[:agg] + (both[agg:] + low)) * scale
                d = rho_new * rho_old * pd[:, sl] + (2.0 * rho_new / DELTA) * z
                pz[:, sl] = z
                pd[:, sl] = d
                px[:, sl] += d
            rho_old = rho_new
        hi, lo = split(px[...])
        m2[:agg, :] = hi
        m2[agg:, :] = lo

    pos = lax.div(me, 2)
    part_rows = agg // PIECES

    def coarse_copy(step, origin, c, peer, sends, recvs):
        at = pl.ds(pl.multiple_of(origin * agg + c * part_rows, part_rows), part_rows)
        return pltpu.make_async_remote_copy(
            src_ref=whole.at[step, at], dst_ref=whole.at[step, at], send_sem=sends, recv_sem=recvs,
            device_id=(grp, peer), device_id_type=MESH,
        )

    def along(step, far_by, way, c, origin):
        peer = me + 2 * far_by if way == UP else me - 2 * far_by
        return coarse_copy(step, origin, c, peer, line_send.at[step, way, far_by - 1, c], line_recv.at[step, way, far_by - 1, c])

    def over(step, c, origin):
        q = lax.div(origin, 2)
        return coarse_copy(step, origin, c, partner, over_send.at[step, q, c], over_recv.at[step, q, c])

    def reaches(far_by, way):
        return pos + far_by < line if way == UP else pos - far_by >= 0

    def gather_open(step):
        for c in range(PIECES):
            over(step, c, me).start()
            for far_by in reversed(range(1, line)):
                for way in (UP, DOWN):
                    @pl.when(reaches(far_by, way))
                    def _():
                        along(step, far_by, way, c, me).start()

    def gather_pass(step):
        for far_by in range(1, line):
            for c in range(PIECES):
                for way in (UP, DOWN):
                    @pl.when(reaches(far_by, 1 - way))
                    def _():
                        origin = me - 2 * far_by if way == UP else me + 2 * far_by
                        along(step, far_by, way, c, origin).wait_recv()
                        over(step, c, origin).start()

    def gather_close(step):
        for c in range(PIECES):
            for q in range(line):
                over(step, c, 2 * q + 1 - odd).wait_recv()
                over(step, c, 2 * q + odd).wait_send()
            for far_by in range(1, line):
                for way in (UP, DOWN):
                    @pl.when(reaches(far_by, way))
                    def _():
                        along(step, far_by, way, c, me).wait_send()

    for way, d in ((0, 1), (1, -1)):
        @pl.when(has[d])
        def _():
            r_copy(way).start()
    mid_product(True)

    def cycle_body(cycle, carry):
        ex = cycle * ROUNDS

        @pl.when(cycle == 0)
        def _():
            for way, d in ((0, 1), (1, -1)):
                @pl.when(has[-d])
                def _():
                    r_copy(way).wait_recv()

                @pl.when(has[d])
                def _():
                    r_copy(way).wait_send()

                hi, lo = split(r_recv[way])
                r2[way, :ghost] = hi
                r2[way, ghost:] = lo

        pair(ex, False)
        whole[cycle, mine, :] = restricted(ex + 1)
        gather_open(cycle)

        gather_pass(cycle)

        @pl.when(cycle == 0)
        def _():
            slab_passes(ends[4], events)
            slab_close()
            take_slabs(max(min(2, ends[3] // CHUNKS + 1), min(3, ends[4] // CHUNKS + 1)), line + 1)
            polynomial()

        gather_close(cycle)
        corr = split_lanes(quads(dot(m2[...], split_lanes(whole[cycle])), agg, width))
        depart(ex + 2, True, 1.0 - OMEGA, OMEGA, dot(go_ref[...], corr))

        def spread(b, c):
            sl = aligned(b * block, block)
            both = dot(oh_ref[pl.ds(pl.multiple_of(ghost + b * block, ghost), block), :], corr)
            t = both[:, :width] + both[:, width:]
            xs[sl, :] = t
            store_ext(ext_v, b, t)
            return c

        lax.fori_loop(0, blocks, spread, 0, unroll=4)
        pair(ex + 2, True)
        pair(ex + 3, False)
        return carry

    lax.fori_loop(0, CYCLES, cycle_body, 0)


def store_kernel(a_ref, b_ref, c_ref, d_ref, sem):
    copies = [pltpu.make_async_copy(a_ref, c_ref, sem.at[0]), pltpu.make_async_copy(b_ref, d_ref, sem.at[1])]
    for copy in copies:
        copy.start()
    for copy in copies:
        copy.wait()


def store(sol, res):
    return pl.pallas_call(
        store_kernel,
        in_specs=[pl.BlockSpec(memory_space=pltpu.VMEM)] * 2,
        out_specs=[pl.BlockSpec(memory_space=pltpu.HBM)] * 2,
        out_shape=[jax.ShapeDtypeStruct(sol.shape, f32)] * 2,
        scratch_shapes=[pltpu.SemaphoreType.DMA((2,))],
        name="store",
    )(*[pltpu.with_memory_space_constraint(x, pltpu.VMEM) for x in (sol, res)])


def body(n_grp, n_sub, right_side, fine_values, columns, agg_map, send_lo, send_hi, coarse_matrix):
    rows, width = right_side.shape
    ghost = send_lo.shape[0]
    block = 2 * ghost
    own = coarse_matrix[0]
    agg, coarse = own.shape
    kept = (coarse // agg // 2 + 1) * agg
    ext_rows = rows + block
    exchanges = CYCLES * ROUNDS
    vmem = pl.BlockSpec(memory_space=pltpu.VMEM)
    field = jax.ShapeDtypeStruct((rows, width), f32)
    dma = pltpu.SemaphoreType.DMA
    sol, res = pl.pallas_call(
        functools.partial(kernel, n_grp, n_sub),
        in_specs=[pl.BlockSpec(memory_space=pltpu.HBM)] * 7,
        out_specs=[vmem] * 2,
        out_shape=[field] * 2,
        scratch_shapes=[
            pltpu.VMEM((rows, width), f32),
            pltpu.VMEM(fine_values.shape, f32),
            pltpu.VMEM(columns.shape, jnp.int32),
            pltpu.VMEM((1, rows), jnp.int32),
            pltpu.VMEM((1, ghost), jnp.int32),
            pltpu.VMEM((1, ghost), jnp.int32),
            pltpu.VMEM((agg, coarse), f32),
            dma((7,)),
            pltpu.VMEM((2 * rows, 2 * block), bf16),
            pltpu.VMEM((rows, block), f32),
            pltpu.VMEM((rows, block), f32),
            pltpu.VMEM((ext_rows, agg), bf16),
            pltpu.VMEM((agg, rows), bf16),
            pltpu.VMEM((6 * ghost, ext_rows), bf16),
            pltpu.VMEM((2 * ghost, ext_rows), f32),
            pltpu.VMEM((2 * ghost, block), f32),
            pltpu.VMEM((rows, width), f32),
            pltpu.VMEM((ext_rows, 2 * width), bf16),
            pltpu.VMEM((ext_rows, 2 * width), bf16),
            pltpu.VMEM((rows, 2 * width), bf16),
            pltpu.VMEM((6 * ghost, 2 * width), f32),
            pltpu.VMEM((exchanges, 2, 2 * ghost, width), f32),
            pltpu.VMEM((exchanges, 2, 2 * ghost, width), f32),
            pltpu.VMEM((exchanges, 2, ghost, width), f32),
            pltpu.VMEM((2, ghost, 2 * ghost), f32),
            pltpu.VMEM((2, ghost, 2 * ghost), f32),
            pltpu.VMEM((2, 2 * ghost, 2 * ghost), bf16),
            dma((exchanges, 2)),
            dma((exchanges, 2)),
            dma((exchanges, 2)),
            dma((exchanges, 2)),
            dma((2,)),
            dma((2,)),
            pltpu.VMEM((coarse, kept), f32),
            dma((2, n_sub // 2, CHUNKS)),
            dma((2, n_sub // 2, CHUNKS)),
            pltpu.VMEM((1, coarse), f32),
            pltpu.VMEM((coarse, coarse), bf16),
            pltpu.VMEM((coarse, coarse), bf16),
            pltpu.VMEM((agg, coarse), f32),
            pltpu.VMEM((agg, coarse), f32),
            pltpu.VMEM((agg, coarse), f32),
            pltpu.VMEM((2 * agg, coarse), bf16),
            pltpu.VMEM((2 * agg, coarse), bf16),
            pltpu.VMEM((CYCLES, coarse, width), f32),
            dma((CYCLES, 2, n_sub // 2 - 1, PIECES)),
            dma((CYCLES, 2, n_sub // 2 - 1, PIECES)),
            dma((CYCLES, n_sub // 2, PIECES)),
            dma((CYCLES, n_sub // 2, PIECES)),
            pltpu.VMEM((6 * ghost, agg), bf16),
        ],
        compiler_params=pltpu.CompilerParams(
            collective_id=0, has_side_effects=True, vmem_limit_bytes=min(60 * 1024 * 1024, 27 * 1024 * 1024 + 9 * coarse * coarse)
        ),
        name="cycles",
    )(*[
        pltpu.with_memory_space_constraint(x, pltpu.HBM)
        for x in (right_side, fine_values, columns, agg_map.reshape(1, rows), send_lo.reshape(1, ghost), send_hi.reshape(1, ghost), own)
    ])
    return store(sol, res)


def solution(mesh):
    placed = (
        P(("grp", "sub"), None),
        P(None, ("grp", "sub")),
        P(None, ("grp", "sub")),
        P(("grp", "sub")),
        P(("grp", "sub")),
        P(("grp", "sub")),
        P("grp", "sub", None),
    )
    return jax.shard_map(
        functools.partial(body, mesh.shape["grp"], mesh.shape["sub"]),
        mesh=mesh,
        in_specs=placed,
        out_specs=(P(("grp", "sub"), None), P(("grp", "sub"), None)),
        check_vma=False,
    )
```

```python
import functools

import jax
import jax.numpy as jnp
from jax import lax
from jax.experimental import pallas as pl
from jax.experimental.pallas import tpu as pltpu
from jax.sharding import PartitionSpec as P

CHEB_COARSE = 6
CYCLES = 2
ROUNDS = 4
FIRST = 3
CHUNKS = 4
PIECES = 2

THETA = 1.0
DELTA = 0.7
OMEGA = 0.6
RHO0 = DELTA / THETA
RHO1 = 1.0 / (2.0 * THETA / DELTA - RHO0)
C1 = RHO1 * RHO0
C2 = 2.0 * RHO1 / DELTA
MESH = pl.DeviceIdType.MESH
f32 = jnp.float32
bf16 = jnp.bfloat16


def split(x):
    hi = x.astype(bf16)
    lo = (x - hi.astype(f32)).astype(bf16)
    return hi, lo


def split_lanes(x):
    hi, lo = split(x)
    return jnp.concatenate([hi, lo], axis=1)


def iota(shape, dim):
    return lax.broadcasted_iota(jnp.int32, shape, dim)


def dot(a, b):
    return jnp.dot(a, b, preferred_element_type=f32)


def quads(product, rows, width):
    return product[:rows, :width] + (product[:rows, width:] + product[rows:, :width])


def aligned(start, size):
    return pl.ds(pl.multiple_of(start, size), size)


def band_tile(fv_ref, col_ref, b, block):
    groups = (fv_ref.shape[0] - 1) // 8
    sl = aligned(b * block, block)
    rows = iota((8, block), 1) + b * block
    cols, vals, firsts = [], [], []
    for i in range(groups):
        cols.append(col_ref[1 + 8 * i : 9 + 8 * i, sl] - rows)
        vals.append(fv_ref[1 + 8 * i : 9 + 8 * i, sl])
    last = jnp.zeros((8, block), f32)
    for i in range(groups):
        last = last + jnp.where(cols[i] == block, vals[i], 0.0)
    last = jnp.sum(last, axis=0, keepdims=True)
    for j in range(groups):
        total = vals[j]
        for i in range(j + 1, groups):
            total = total + jnp.where(cols[i] == cols[j], vals[i], 0.0)
        firsts.append(total)
    high_count = block // 8
    places = [iota((8, block), 0) + 8 * h for h in range(high_count)]
    sums = [jnp.zeros((8, block), f32)] * high_count
    for s in range(8):
        chains = [jnp.zeros((8, block), f32)] * high_count
        for i in reversed(range(groups)):
            col = jnp.broadcast_to(cols[i][s : s + 1, :], (8, block))
            val = jnp.broadcast_to(firsts[i][s : s + 1, :], (8, block))
            chains = [jnp.where(col == places[h], val, chains[h]) for h in range(high_count)]
        sums = [sums[h] + chains[h] for h in range(high_count)]
    by_offset = jnp.concatenate(sums, axis=0).T
    skewed = pltpu.roll(by_offset, 0, 1, stride=1, stride_axis=0)
    lane = iota((block, block), 1)
    sub = iota((block, block), 0)
    low = jnp.where(lane >= sub, skewed, 0.0)
    high = jnp.where(lane < sub, skewed, jnp.where(lane == sub, last, 0.0))
    return low, high


def kernel(n_grp, n_sub, *refs):
    ins = refs[:7]
    (sol_ref, res_ref,
     rhs_ref, fv_ref, col_ref, agg_ref, lo_ref, hi_ref, own_ref, in_sem,
     a2, dinv_ref, diag_ref, oh_ref, oht_ref, g_ref, sa, dinv_s,
     xs, ext_v, ext_w, s2, y_mid,
     send, recv, far, r_send, r_recv, r2,
     send_sem, recv_sem, far_send_sem, far_recv_sem, r_send_sem, r_recv_sem,
     slabs, slab_send_sem, slab_recv_sem, cinv_ref, m_hi, m_lo, pd, pz, px, pair2, m2,
     whole, line_send, line_recv, over_send, over_recv, go_ref) = refs[7:]
    held = (rhs_ref, fv_ref, col_ref, agg_ref, lo_ref, hi_ref, own_ref)
    loads = [pltpu.make_async_copy(ins[i], held[i], in_sem.at[i]) for i in range(7)]
    for i in (6, 1, 2, 4, 5, 0, 3):
        loads[i].start()
    rows_dev, width = rhs_ref.shape
    ghost = lo_ref.shape[1]
    block = 2 * ghost
    blocks = rows_dev // block
    agg, coarse = own_ref.shape
    parts = coarse // agg
    kept = slabs.shape[1]
    grp = lax.axis_index("grp")
    me = lax.axis_index("sub")
    total = n_grp * n_sub
    part = grp * n_sub + me
    ones = functools.partial(jnp.asarray, dtype=jnp.int32)

    def device(p):
        return lax.div(p, n_sub), lax.rem(p, n_sub)

    has = {d: jnp.logical_and(part + d >= 0, part + d < total) for d in (1, -1, 2, -2)}

    barrier = pltpu.get_barrier_semaphore()
    for j in range(1, n_sub):
        pl.semaphore_signal(barrier, inc=1, device_id=(grp, lax.rem(me + j, n_sub)), device_id_type=MESH)
    greeted = n_sub - 1
    for d in (1, -1, 2, -2):
        outside = jnp.logical_or(me + d < 0, me + d >= n_sub)
        across = jnp.logical_and(has[d], outside)

        @pl.when(across)
        def _():
            pl.semaphore_signal(barrier, inc=1, device_id=device(part + d), device_id_type=MESH)

        greeted = greeted + across.astype(jnp.int32)

    mine = aligned(me * agg, agg)
    loads[6].wait()
    for k in range(kept // agg):
        slabs[mine, k * agg : (k + 1) * agg] = own_ref[:, aligned(lax.rem(me + k, n_sub) * agg, agg)]
    pl.semaphore_wait(barrier, greeted)

    line = n_sub // 2
    odd = lax.rem(me, 2)
    partner = me + 1 - 2 * odd
    place = jnp.where(odd == 1, lax.div(me, 2), n_sub - 1 - lax.div(me, 2))
    chunk = agg // CHUNKS
    halved = CHUNKS // 2
    UP, DOWN = range(2)

    def at_place(q):
        q = lax.rem(q + n_sub, n_sub)
        return jnp.where(q < line, 2 * q + 1, 2 * (n_sub - 1 - q))

    def origin_of(step, way):
        return at_place(place - step if way == UP else place + step)

    def slab(origin, step, c, way, act):
        peer = at_place(place + 1 if way == UP else place - 1)

        def copy(columns):
            at = pl.ds(pl.multiple_of(origin * agg + c * chunk, chunk), chunk)
            act(pltpu.make_async_remote_copy(
                src_ref=slabs.at[at, pl.ds(0, columns)], dst_ref=slabs.at[at, pl.ds(0, columns)],
                send_sem=slab_send_sem.at[way, step, c], recv_sem=slab_recv_sem.at[way, step, c],
                device_id=(grp, peer), device_id_type=MESH,
            ))

        @pl.when(origin < line)
        def _():
            copy(kept)

        @pl.when(origin >= line)
        def _():
            copy(kept - agg)

    def start(copy):
        copy.start()

    def wait_send(copy):
        copy.wait_send()

    def wait_recv(copy):
        copy.wait_recv()

    def slab_open():
        def one(c, carry):
            for way in (UP, DOWN):
                slab(me, 0, c, way, start)
            return carry

        lax.fori_loop(0, CHUNKS, one, 0)

    events = (line - 1) * CHUNKS + halved

    def slab_passes(first, last):
        def one(event, carry):
            step = lax.div(event, CHUNKS)
            c = lax.rem(event, CHUNKS)
            for way in (UP, DOWN):
                at = c if way == UP else lax.rem(c + halved, CHUNKS)
                origin = origin_of(step + 1, way)
                slab(origin, step, at, way, wait_recv)

                @pl.when(event + CHUNKS < (line - 1) * CHUNKS + halved)
                def _():
                    slab(origin, step + 1, at, way, start)

            return carry

        lax.fori_loop(first, last, one, 0)

    def slab_close():
        def one(event, carry):
            step = lax.div(event, CHUNKS)
            c = lax.rem(event, CHUNKS)
            for way in (UP, DOWN):
                slab(origin_of(step, way), step, c if way == UP else lax.rem(c + halved, CHUNKS), way, wait_send)
            return carry

        lax.fori_loop(0, events, one, 0)

    half = parts // 2
    eye = iota((agg, agg), 0) == iota((agg, agg), 1)

    def take_slab(j):
        sl = aligned(j * agg, agg)
        cinv_ref[:, sl] = 1.0 / jnp.sum(jnp.where(eye, slabs[sl, :agg], 0.0), axis=0, keepdims=True)

        def place_tile(k):
            so = aligned(lax.rem(j + k, parts) * agg, agg)
            tile = slabs[sl, k * agg : (k + 1) * agg]
            m_hi[sl, so], m_lo[sl, so] = split(tile)
            if k:
                m_hi[so, sl], m_lo[so, sl] = split(tile.T)

        for k in range(half):
            place_tile(k)

        @pl.when(j < half)
        def _():
            place_tile(half)

    def take_slabs(first, last):
        def one(step, carry):
            take_slab(origin_of(step, UP))

            @pl.when(jnp.logical_and(step > 0, step < line))
            def _():
                take_slab(origin_of(step, DOWN))

            return carry

        lax.fori_loop(first, last, one, 0)

    slab_open()

    for d, slot in ((-1, 0), (1, 1)):
        @pl.when(jnp.logical_not(has[d]))
        def _():
            recv[:, slot] = jnp.zeros((recv.shape[0],) + recv.shape[2:], f32)
            r_recv[slot] = jnp.zeros(r_recv.shape[1:], f32)

    for d, slot in ((-2, 0), (2, 1)):
        @pl.when(jnp.logical_not(has[d]))
        def _():
            far[:, slot] = jnp.zeros((far.shape[0],) + far.shape[2:], f32)

    for ext in (ext_v, ext_w):
        ext[:ghost, :] = jnp.zeros((ghost, 2 * width), bf16)
        ext[ghost + rows_dev :, :] = jnp.zeros((ghost, 2 * width), bf16)
    for i in (1, 2, 4, 5, 0, 3):
        loads[i].wait()
    sent_row = jnp.concatenate([hi_ref[...], lo_ref[...]], axis=1).astype(f32)
    sent = jnp.broadcast_to(sent_row, (2 * ghost, 2 * ghost)).T.astype(jnp.int32)
    lane = iota((2 * ghost, block), 1)
    for j in range(blocks + 1):
        g_ref[: 2 * ghost, j * block : (j + 1) * block] = (sent + (ghost - j * block) == lane).astype(f32).astype(bf16)
    dinv_s[...] = jnp.zeros_like(dinv_s)
    oh_ref[:ghost, :] = jnp.zeros((ghost, agg), bf16)
    oh_ref[ghost + rows_dev :, :] = jnp.zeros((ghost, agg), bf16)
    sa[:, :block] = jnp.zeros((2 * ghost, block), f32)

    def fine(b):
        sl = aligned(b * block, block)
        low, high = band_tile(fv_ref, col_ref, b, block)
        diag = jnp.broadcast_to(fv_ref[0:1, sl], (block, block)).T
        dinv = 1.0 / diag
        diag_ref[sl, :] = diag
        dinv_ref[sl, :] = dinv
        for at, tile in ((0, low), (block, high)):
            hi, lo = split(tile)
            a2[aligned(b * 2 * block, block), at : at + block] = hi
            a2[aligned(b * 2 * block + block, block), at : at + block] = lo
        rhs = rhs_ref[sl, :]
        res_ref[sl, :] = rhs
        sol_ref[sl, :] = jnp.zeros_like(rhs)
        v = dinv * rhs
        xs[sl, :] = v
        ext_v[pl.ds(pl.multiple_of(ghost + b * block, ghost), block), :] = split_lanes(v)

    def setup(i, carry):
        for u in range(2):
            fine(2 * i + u)
        slab_passes(jnp.clip(i - FIRST, 0, events), jnp.clip(i + 1 - FIRST, 0, events))
        return carry

    lax.fori_loop(0, blocks // 2, setup, 0)
    done = min(blocks // 2 - FIRST, events)
    ends = [done] + [min(done + n, events) for n in (0, 2, 3, 5)]

    def sent_rows(b, carry):
        sl = aligned(b * block, block)
        onehot = (iota((agg, block), 0) == agg_ref[:, sl]).astype(f32)
        oht_ref[:, sl] = onehot.astype(bf16)
        oh_ref[pl.ds(pl.multiple_of(ghost + b * block, ghost), block), :] = onehot.T.astype(bf16)
        picked = (sent - b * block == lane).astype(f32).astype(bf16)
        both = dot(picked, a2[aligned(b * 2 * block, block), :]) + dot(picked, a2[aligned(b * 2 * block + block, block), :])
        sa[:, sl] = sa[:, sl] + both[:, :block]
        sa[:, aligned((b + 1) * block, block)] = both[:, block:]
        both = dot(picked, split_lanes(dinv_ref[sl, :]))
        dinv_s[...] += both[:, :block] + both[:, block:]
        return carry

    lax.fori_loop(0, blocks, sent_rows, 0, unroll=4)
    slab_passes(ends[0], ends[1])
    for j in range(blocks + 1):
        at = slice(j * block, (j + 1) * block)
        scaled = sa[:, at] * dinv_s[...]
        g_ref[2 * ghost : 4 * ghost, at], g_ref[4 * ghost :, at] = split(scaled)
        if j == 0:
            below = scaled
    spread_sent = dot(g_ref[...], oh_ref[...])
    go_ref[: 2 * ghost] = spread_sent[: 2 * ghost].astype(bf16)
    go_ref[2 * ghost : 4 * ghost], go_ref[4 * ghost :] = split(spread_sent[2 * ghost : 4 * ghost] + spread_sent[4 * ghost :])
    response = jnp.where(lane < ghost, below, scaled)
    r_send[0] = response[:ghost]
    r_send[1] = response[ghost:]

    def r_copy(way):
        d = (1, -1)[way]
        return pltpu.make_async_remote_copy(
            src_ref=r_send.at[way], dst_ref=r_recv.at[way],
            send_sem=r_send_sem.at[way], recv_sem=r_recv_sem.at[way],
            device_id=device(part + d), device_id_type=MESH,
        )

    def near_copy(ex, way, count):
        d = (1, -1)[way]
        return pltpu.make_async_remote_copy(
            src_ref=send.at[ex, way, pl.ds(0, count)], dst_ref=recv.at[ex, way, pl.ds(0, count)],
            send_sem=send_sem.at[ex, way], recv_sem=recv_sem.at[ex, way],
            device_id=device(part + d), device_id_type=MESH,
        )

    def far_copy(ex, way):
        d = (2, -2)[way]
        return pltpu.make_async_remote_copy(
            src_ref=send.at[ex, way, pl.ds(0, ghost)], dst_ref=far.at[ex, way],
            send_sem=far_send_sem.at[ex, way], recv_sem=far_recv_sem.at[ex, way],
            device_id=device(part + d), device_id_type=MESH,
        )

    def mid_product(double):
        high = 6 * ghost if double else 2 * ghost
        inner = slice(2 * block, (blocks - 1) * block)
        y_mid[:high] = dot(g_ref[:high, inner], ext_v[inner, :])

    def all_sent(double):
        high = 6 * ghost if double else 2 * ghost
        y = y_mid[:high]
        for rim in (slice(0, 2 * block), slice((blocks - 1) * block, (blocks + 1) * block)):
            y = y + dot(g_ref[:high, rim], ext_v[rim, :])
        return y

    def depart(ex, double, alpha, beta, y):
        now = y[: 2 * ghost, :width] + y[: 2 * ghost, width:]
        for way in range(2):
            send[ex, way, :ghost] = now[way * ghost : (way + 1) * ghost]
        if double:
            later = alpha * now - beta * quads(y[2 * ghost :], 2 * ghost, width)
            for way in range(2):
                send[ex, way, ghost:] = later[way * ghost : (way + 1) * ghost]
        for way, d in ((0, 1), (1, -1)):
            @pl.when(has[d])
            def _():
                near_copy(ex, way, 2 * ghost if double else ghost).start()
        if double:
            for way, d in ((0, 2), (1, -2)):
                @pl.when(has[d])
                def _():
                    far_copy(ex, way).start()

    def arrive(ex, double):
        count = 2 * ghost if double else ghost
        for way, d in ((0, 1), (1, -1)):
            @pl.when(has[-d])
            def _():
                near_copy(ex, way, count).wait_recv()

            @pl.when(has[d])
            def _():
                near_copy(ex, way, count).wait_send()
        if double:
            for way, d in ((0, 2), (1, -2)):
                @pl.when(has[-d])
                def _():
                    far_copy(ex, way).wait_recv()

                @pl.when(has[d])
                def _():
                    far_copy(ex, way).wait_send()

    def local_apply(ext, fn):
        def go(b, carry):
            a = a2[aligned(b * 2 * block, 2 * block), :]
            x = ext[pl.ds(pl.multiple_of(b * block, block), 2 * block), :]
            fn(b, aligned(b * block, block), quads(dot(a, x), block, width))
            return carry

        lax.fori_loop(0, blocks, go, 0, unroll=8)

    def store_ext(ext, b, x):
        ext[pl.ds(pl.multiple_of(ghost + b * block, ghost), block), :] = split_lanes(x)

    last_tile = (blocks - 1) * 2 * block
    below_rows = slice(0, ghost)
    above_rows = slice(rows_dev - ghost, rows_dev)

    def ghost_terms(ex):
        nothing = jnp.zeros((ghost, 2 * width), bf16)
        a_below = jnp.concatenate([a2[:ghost, :block], a2[block : block + ghost, :block]], axis=0)
        a_above = jnp.concatenate(
            [a2[last_tile + ghost : last_tile + block, block:], a2[last_tile + block + ghost : last_tile + 2 * block, block:]],
            axis=0,
        )
        from_below = jnp.concatenate([split_lanes(recv[ex, 0, :ghost]), nothing], axis=0)
        from_above = jnp.concatenate([nothing, split_lanes(recv[ex, 1, :ghost])], axis=0)
        return quads(dot(a_below, from_below), ghost, width), quads(dot(a_above, from_above), ghost, width)

    def pair(ex, te):
        alpha, beta = (1.0 - OMEGA, OMEGA) if te else (C1, C2)
        gamma = OMEGA if te else C2 - 1.0
        if not te:
            depart(ex, True, alpha, beta, all_sent(True))

        def first(b, sl, off):
            v = xs[sl, :]
            w = alpha * v - beta * (dinv_ref[sl, :] * off)
            store_ext(ext_w, b, w)
            r = res_ref[sl, :]
            if te:
                res_ref[sl, :] = r - alpha * (diag_ref[sl, :] * v) + gamma * off
                sol_ref[sl, :] += w
            else:
                res_ref[sl, :] = gamma * off - alpha * r
                sol_ref[sl, :] += v + w

        local_apply(ext_v, first)
        if not te:
            @pl.when(ex == 0)
            def _():
                slab_passes(ends[1], ends[2])

        def second(b, sl, off):
            r = res_ref[sl, :] - off
            res_ref[sl, :] = r
            v = dinv_ref[sl, :] * r
            xs[sl, :] = v
            store_ext(ext_v, b, v)

        local_apply(ext_w, second)
        mid_product(True)
        if not te:
            @pl.when(ex == 0)
            def _():
                slab_passes(ends[2], ends[3])
                take_slabs(0, min(2, ends[3] // CHUNKS + 1))

        arrive(ex, True)
        off_below, off_above = ghost_terms(ex)
        dw_below = -beta * (dinv_ref[below_rows, :] * off_below)
        dw_above = -beta * (dinv_ref[above_rows, :] * off_above)
        seen_below = jnp.concatenate([split_lanes(far[ex, 0]), split_lanes(send[ex, 1, :ghost])], axis=0)
        seen_above = jnp.concatenate([split_lanes(send[ex, 0, :ghost]), split_lanes(far[ex, 1])], axis=0)
        next_below = recv[ex, 0, ghost:] - beta * quads(dot(r2[0], seen_below), ghost, width)
        next_above = recv[ex, 1, ghost:] - beta * quads(dot(r2[1], seen_above), ghost, width)
        add_below = jnp.concatenate([split_lanes(next_below), split_lanes(dw_below)], axis=0)
        add_above = jnp.concatenate([split_lanes(dw_above), split_lanes(next_above)], axis=0)
        more_below = quads(dot(a2[: 2 * block, :block], add_below), block, width)
        more_above = quads(dot(a2[last_tile:, block:], add_above), block, width)
        zero = jnp.zeros((ghost, width), f32)
        dr_below = jnp.concatenate([gamma * off_below, zero], axis=0) - more_below
        dr_above = jnp.concatenate([zero, gamma * off_above], axis=0) - more_above
        sol_ref[below_rows, :] += dw_below
        sol_ref[above_rows, :] += dw_above
        for b, dr in ((0, dr_below), (blocks - 1, dr_above)):
            sl = slice(b * block, (b + 1) * block)
            r = res_ref[sl, :] + dr
            res_ref[sl, :] = r
            v = dinv_ref[sl, :] * r
            xs[sl, :] = v
            ext_v[ghost + b * block : ghost + (b + 1) * block, :] = split_lanes(v)

    def restricted(ex):
        depart(ex, False, 0.0, 0.0, all_sent(False))

        def restrict(b, sl, off):
            s2[sl, :] = split_lanes((1.0 - OMEGA) * res_ref[sl, :] - OMEGA * off)

        local_apply(ext_v, restrict)
        both = dot(oht_ref[...], s2[...])

        @pl.when(ex == 1)
        def _():
            slab_passes(ends[3], ends[4])
            taken = min(2, ends[3] // CHUNKS + 1)
            take_slabs(taken, max(taken, min(3, ends[4] // CHUNKS + 1)))

        arrive(ex, False)
        off_below, off_above = ghost_terms(ex)
        nothing = jnp.zeros((ghost, 2 * width), bf16)
        ds_below = jnp.concatenate([split_lanes(-OMEGA * off_below), nothing], axis=0)
        ds_above = jnp.concatenate([nothing, split_lanes(-OMEGA * off_above)], axis=0)
        both = both + dot(oht_ref[:, :block], ds_below) + dot(oht_ref[:, rows_dev - block :], ds_above)
        return both[:, :width] + both[:, width:]

    def polynomial():
        cinv = [cinv_ref[:, j * agg : (j + 1) * agg] for j in range(parts)]
        first_rho = 1.0 / (2.0 * THETA / DELTA - RHO0)
        mine_diag = own_ref[:, mine]
        mine_inv = 1.0 / jnp.sum(jnp.where(eye, mine_diag, 0.0), axis=1, keepdims=True)
        for j in range(parts):
            sl = slice(j * agg, (j + 1) * agg)
            begin = jnp.where(jnp.logical_and(eye, me == j), cinv[j], 0.0)
            z = begin - (mine_inv * own_ref[:, sl]) * cinv[j]
            d = first_rho * RHO0 * begin + (2.0 * first_rho / DELTA) * z
            pz[:, sl] = z
            pd[:, sl] = d
            px[:, sl] = begin + d
        rho_old = first_rho
        for turn in range(2, CHEB_COARSE):
            rho_new = 1.0 / (2.0 * THETA / DELTA - rho_old)
            hi, lo = split(pd[...])
            pair2[:agg, :] = hi
            pair2[agg:, :] = lo
            for j in range(parts // 2):
                sl = slice(2 * j * agg, (2 * j + 2) * agg)
                both = dot(pair2[...], m_hi[:, sl])
                low = dot(pair2[:agg, :], m_lo[:, sl])
                scale = jnp.concatenate([cinv[2 * j], cinv[2 * j + 1]], axis=1)
                z = pz[:, sl] - (both[:agg] + (both[agg:] + low)) * scale
                d = rho_new * rho_old * pd[:, sl] + (2.0 * rho_new / DELTA) * z
                pz[:, sl] = z
                pd[:, sl] = d
                px[:, sl] += d
            rho_old = rho_new
        hi, lo = split(px[...])
        m2[:agg, :] = hi
        m2[agg:, :] = lo

    pos = lax.div(me, 2)
    part_rows = agg // PIECES

    def coarse_copy(step, origin, c, peer, sends, recvs):
        at = pl.ds(pl.multiple_of(origin * agg + c * part_rows, part_rows), part_rows)
        return pltpu.make_async_remote_copy(
            src_ref=whole.at[step, at], dst_ref=whole.at[step, at], send_sem=sends, recv_sem=recvs,
            device_id=(grp, peer), device_id_type=MESH,
        )

    def along(step, far_by, way, c, origin):
        peer = me + 2 * far_by if way == UP else me - 2 * far_by
        return coarse_copy(step, origin, c, peer, line_send.at[step, way, far_by - 1, c], line_recv.at[step, way, far_by - 1, c])

    def over(step, c, origin):
        q = lax.div(origin, 2)
        return coarse_copy(step, origin, c, partner, over_send.at[step, q, c], over_recv.at[step, q, c])

    def reaches(far_by, way):
        return pos + far_by < line if way == UP else pos - far_by >= 0

    def gather_open(step):
        for c in range(PIECES):
            over(step, c, me).start()
            for far_by in reversed(range(1, line)):
                for way in (UP, DOWN):
                    @pl.when(reaches(far_by, way))
                    def _():
                        along(step, far_by, way, c, me).start()

    def gather_pass(step):
        for far_by in range(1, line):
            for c in range(PIECES):
                for way in (UP, DOWN):
                    @pl.when(reaches(far_by, 1 - way))
                    def _():
                        origin = me - 2 * far_by if way == UP else me + 2 * far_by
                        along(step, far_by, way, c, origin).wait_recv()
                        over(step, c, origin).start()

    def gather_close(step):
        for c in range(PIECES):
            for q in range(line):
                over(step, c, 2 * q + 1 - odd).wait_recv()
                over(step, c, 2 * q + odd).wait_send()
            for far_by in range(1, line):
                for way in (UP, DOWN):
                    @pl.when(reaches(far_by, way))
                    def _():
                        along(step, far_by, way, c, me).wait_send()

    for way, d in ((0, 1), (1, -1)):
        @pl.when(has[d])
        def _():
            r_copy(way).start()
    mid_product(True)

    def cycle_body(cycle, carry):
        ex = cycle * ROUNDS

        @pl.when(cycle == 0)
        def _():
            for way, d in ((0, 1), (1, -1)):
                @pl.when(has[-d])
                def _():
                    r_copy(way).wait_recv()

                @pl.when(has[d])
                def _():
                    r_copy(way).wait_send()

                hi, lo = split(r_recv[way])
                r2[way, :ghost] = hi
                r2[way, ghost:] = lo

        pair(ex, False)
        whole[cycle, mine, :] = restricted(ex + 1)
        gather_open(cycle)

        gather_pass(cycle)

        @pl.when(cycle == 0)
        def _():
            slab_passes(ends[4], events)
            slab_close()
            take_slabs(max(min(2, ends[3] // CHUNKS + 1), min(3, ends[4] // CHUNKS + 1)), line + 1)
            polynomial()

        gather_close(cycle)
        corr = split_lanes(quads(dot(m2[...], split_lanes(whole[cycle])), agg, width))
        depart(ex + 2, True, 1.0 - OMEGA, OMEGA, dot(go_ref[...], corr))

        def spread(b, c):
            sl = aligned(b * block, block)
            both = dot(oh_ref[pl.ds(pl.multiple_of(ghost + b * block, ghost), block), :], corr)
            t = both[:, :width] + both[:, width:]
            xs[sl, :] = t
            store_ext(ext_v, b, t)
            return c

        lax.fori_loop(0, blocks, spread, 0, unroll=4)
        pair(ex + 2, True)
        pair(ex + 3, False)
        return carry

    lax.fori_loop(0, CYCLES, cycle_body, 0)


def store_kernel(a_ref, b_ref, c_ref, d_ref, sem):
    copies = [pltpu.make_async_copy(a_ref, c_ref, sem.at[0]), pltpu.make_async_copy(b_ref, d_ref, sem.at[1])]
    for copy in copies:
        copy.start()
    for copy in copies:
        copy.wait()


def store(sol, res):
    return pl.pallas_call(
        store_kernel,
        in_specs=[pl.BlockSpec(memory_space=pltpu.VMEM)] * 2,
        out_specs=[pl.BlockSpec(memory_space=pltpu.HBM)] * 2,
        out_shape=[jax.ShapeDtypeStruct(sol.shape, f32)] * 2,
        scratch_shapes=[pltpu.SemaphoreType.DMA((2,))],
        name="store",
    )(*[pltpu.with_memory_space_constraint(x, pltpu.VMEM) for x in (sol, res)])


def body(n_grp, n_sub, right_side, fine_values, columns, agg_map, send_lo, send_hi, coarse_matrix):
    rows, width = right_side.shape
    ghost = send_lo.shape[0]
    block = 2 * ghost
    own = coarse_matrix[0]
    agg, coarse = own.shape
    kept = (coarse // agg // 2 + 1) * agg
    ext_rows = rows + block
    exchanges = CYCLES * ROUNDS
    vmem = pl.BlockSpec(memory_space=pltpu.VMEM)
    field = jax.ShapeDtypeStruct((rows, width), f32)
    dma = pltpu.SemaphoreType.DMA
    sol, res = pl.pallas_call(
        functools.partial(kernel, n_grp, n_sub),
        in_specs=[pl.BlockSpec(memory_space=pltpu.HBM)] * 7,
        out_specs=[vmem] * 2,
        out_shape=[field] * 2,
        scratch_shapes=[
            pltpu.VMEM((rows, width), f32),
            pltpu.VMEM(fine_values.shape, f32),
            pltpu.VMEM(columns.shape, jnp.int32),
            pltpu.VMEM((1, rows), jnp.int32),
            pltpu.VMEM((1, ghost), jnp.int32),
            pltpu.VMEM((1, ghost), jnp.int32),
            pltpu.VMEM((agg, coarse), f32),
            dma((7,)),
            pltpu.VMEM((2 * rows, 2 * block), bf16),
            pltpu.VMEM((rows, block), f32),
            pltpu.VMEM((rows, block), f32),
            pltpu.VMEM((ext_rows, agg), bf16),
            pltpu.VMEM((agg, rows), bf16),
            pltpu.VMEM((6 * ghost, ext_rows), bf16),
            pltpu.VMEM((2 * ghost, ext_rows), f32),
            pltpu.VMEM((2 * ghost, block), f32),
            pltpu.VMEM((rows, width), f32),
            pltpu.VMEM((ext_rows, 2 * width), bf16),
            pltpu.VMEM((ext_rows, 2 * width), bf16),
            pltpu.VMEM((rows, 2 * width), bf16),
            pltpu.VMEM((6 * ghost, 2 * width), f32),
            pltpu.VMEM((exchanges, 2, 2 * ghost, width), f32),
            pltpu.VMEM((exchanges, 2, 2 * ghost, width), f32),
            pltpu.VMEM((exchanges, 2, ghost, width), f32),
            pltpu.VMEM((2, ghost, 2 * ghost), f32),
            pltpu.VMEM((2, ghost, 2 * ghost), f32),
            pltpu.VMEM((2, 2 * ghost, 2 * ghost), bf16),
            dma((exchanges, 2)),
            dma((exchanges, 2)),
            dma((exchanges, 2)),
            dma((exchanges, 2)),
            dma((2,)),
            dma((2,)),
            pltpu.VMEM((coarse, kept), f32),
            dma((2, n_sub // 2, CHUNKS)),
            dma((2, n_sub // 2, CHUNKS)),
            pltpu.VMEM((1, coarse), f32),
            pltpu.VMEM((coarse, coarse), bf16),
            pltpu.VMEM((coarse, coarse), bf16),
            pltpu.VMEM((agg, coarse), f32),
            pltpu.VMEM((agg, coarse), f32),
            pltpu.VMEM((agg, coarse), f32),
            pltpu.VMEM((2 * agg, coarse), bf16),
            pltpu.VMEM((2 * agg, coarse), bf16),
            pltpu.VMEM((CYCLES, coarse, width), f32),
            dma((CYCLES, 2, n_sub // 2 - 1, PIECES)),
            dma((CYCLES, 2, n_sub // 2 - 1, PIECES)),
            dma((CYCLES, n_sub // 2, PIECES)),
            dma((CYCLES, n_sub // 2, PIECES)),
            pltpu.VMEM((6 * ghost, agg), bf16),
        ],
        compiler_params=pltpu.CompilerParams(
            collective_id=0, has_side_effects=True, vmem_limit_bytes=min(60 * 1024 * 1024, 27 * 1024 * 1024 + 9 * coarse * coarse)
        ),
        name="cycles",
    )(*[
        pltpu.with_memory_space_constraint(x, pltpu.HBM)
        for x in (right_side, fine_values, columns, agg_map.reshape(1, rows), send_lo.reshape(1, ghost), send_hi.reshape(1, ghost), own)
    ])
    return store(sol, res)


def solution(mesh):
    placed = (
        P(("grp", "sub"), None),
        P(None, ("grp", "sub")),
        P(None, ("grp", "sub")),
        P(("grp", "sub")),
        P(("grp", "sub")),
        P(("grp", "sub")),
        P("grp", "sub", None),
    )
    return jax.shard_map(
        functools.partial(body, mesh.shape["grp"], mesh.shape["sub"]),
        mesh=mesh,
        in_specs=placed,
        out_specs=(P(("grp", "sub"), None), P(("grp", "sub"), None)),
        check_vma=False,
    )
```

```python
import functools

import jax
import jax.numpy as jnp
from jax import lax
from jax.experimental import pallas as pl
from jax.experimental.pallas import tpu as pltpu
from jax.sharding import PartitionSpec as P

CHEB_COARSE = 6
CYCLES = 2
ROUNDS = 4
FIRST = 3
CHUNKS = 4
PIECES = 2

THETA = 1.0
DELTA = 0.7
OMEGA = 0.6
RHO0 = DELTA / THETA
RHO1 = 1.0 / (2.0 * THETA / DELTA - RHO0)
C1 = RHO1 * RHO0
C2 = 2.0 * RHO1 / DELTA
MESH = pl.DeviceIdType.MESH
f32 = jnp.float32
bf16 = jnp.bfloat16


def split(x):
    hi = x.astype(bf16)
    lo = (x - hi.astype(f32)).astype(bf16)
    return hi, lo


def split_lanes(x):
    hi, lo = split(x)
    return jnp.concatenate([hi, lo], axis=1)


def iota(shape, dim):
    return lax.broadcasted_iota(jnp.int32, shape, dim)


def dot(a, b):
    return jnp.dot(a, b, preferred_element_type=f32)


def quads(product, rows, width):
    return product[:rows, :width] + (product[:rows, width:] + product[rows:, :width])


def aligned(start, size):
    return pl.ds(pl.multiple_of(start, size), size)


def band_tile(fv_ref, col_ref, b, block):
    groups = (fv_ref.shape[0] - 1) // 8
    sl = aligned(b * block, block)
    rows = iota((8, block), 1) + b * block
    cols, vals, firsts = [], [], []
    for i in range(groups):
        cols.append(col_ref[1 + 8 * i : 9 + 8 * i, sl] - rows)
        vals.append(fv_ref[1 + 8 * i : 9 + 8 * i, sl])
    last = jnp.zeros((8, block), f32)
    for i in range(groups):
        last = last + jnp.where(cols[i] == block, vals[i], 0.0)
    last = jnp.sum(last, axis=0, keepdims=True)
    for j in range(groups):
        total = vals[j]
        for i in range(j + 1, groups):
            total = total + jnp.where(cols[i] == cols[j], vals[i], 0.0)
        firsts.append(total)
    high_count = block // 8
    places = [iota((8, block), 0) + 8 * h for h in range(high_count)]
    sums = [jnp.zeros((8, block), f32)] * high_count
    for s in range(8):
        chains = [jnp.zeros((8, block), f32)] * high_count
        for i in reversed(range(groups)):
            col = jnp.broadcast_to(cols[i][s : s + 1, :], (8, block))
            val = jnp.broadcast_to(firsts[i][s : s + 1, :], (8, block))
            chains = [jnp.where(col == places[h], val, chains[h]) for h in range(high_count)]
        sums = [sums[h] + chains[h] for h in range(high_count)]
    by_offset = jnp.concatenate(sums, axis=0).T
    skewed = pltpu.roll(by_offset, 0, 1, stride=1, stride_axis=0)
    lane = iota((block, block), 1)
    sub = iota((block, block), 0)
    low = jnp.where(lane >= sub, skewed, 0.0)
    high = jnp.where(lane < sub, skewed, jnp.where(lane == sub, last, 0.0))
    return low, high


def kernel(n_grp, n_sub, *refs):
    ins = refs[:7]
    (sol_ref, res_ref,
     rhs_ref, fv_ref, col_ref, agg_ref, lo_ref, hi_ref, own_ref, in_sem,
     a2, dinv_ref, diag_ref, oh_ref, oht_ref, g_ref, sa, dinv_s,
     xs, ext_v, ext_w, s2, y_mid,
     send, recv, far, r_send, r_recv, r2,
     send_sem, recv_sem, far_send_sem, far_recv_sem, r_send_sem, r_recv_sem,
     slabs, slab_send_sem, slab_recv_sem, cinv_ref, m_hi, m_lo, pd, pz, px, pair2, m2,
     whole, line_send, line_recv, over_send, over_recv, go_ref) = refs[7:]
    held = (rhs_ref, fv_ref, col_ref, agg_ref, lo_ref, hi_ref, own_ref)
    loads = [pltpu.make_async_copy(ins[i], held[i], in_sem.at[i]) for i in range(7)]
    for i in (6, 1, 2, 4, 5, 0, 3):
        loads[i].start()
    rows_dev, width = rhs_ref.shape
    ghost = lo_ref.shape[1]
    block = 2 * ghost
    blocks = rows_dev // block
    agg, coarse = own_ref.shape
    parts = coarse // agg
    kept = slabs.shape[1]
    grp = lax.axis_index("grp")
    me = lax.axis_index("sub")
    total = n_grp * n_sub
    part = grp * n_sub + me
    ones = functools.partial(jnp.asarray, dtype=jnp.int32)

    def device(p):
        return lax.div(p, n_sub), lax.rem(p, n_sub)

    has = {d: jnp.logical_and(part + d >= 0, part + d < total) for d in (1, -1, 2, -2)}

    barrier = pltpu.get_barrier_semaphore()
    for j in range(1, n_sub):
        pl.semaphore_signal(barrier, inc=1, device_id=(grp, lax.rem(me + j, n_sub)), device_id_type=MESH)
    greeted = n_sub - 1
    for d in (1, -1, 2, -2):
        outside = jnp.logical_or(me + d < 0, me + d >= n_sub)
        across = jnp.logical_and(has[d], outside)

        @pl.when(across)
        def _():
            pl.semaphore_signal(barrier, inc=1, device_id=device(part + d), device_id_type=MESH)

        greeted = greeted + across.astype(jnp.int32)

    mine = aligned(me * agg, agg)
    loads[6].wait()
    for k in range(kept // agg):
        slabs[mine, k * agg : (k + 1) * agg] = own_ref[:, aligned(lax.rem(me + k, n_sub) * agg, agg)]
    pl.semaphore_wait(barrier, greeted)

    line = n_sub // 2
    odd = lax.rem(me, 2)
    partner = me + 1 - 2 * odd
    place = jnp.where(odd == 1, lax.div(me, 2), n_sub - 1 - lax.div(me, 2))
    chunk = agg // CHUNKS
    halved = CHUNKS // 2
    UP, DOWN = range(2)

    def at_place(q):
        q = lax.rem(q + n_sub, n_sub)
        return jnp.where(q < line, 2 * q + 1, 2 * (n_sub - 1 - q))

    def origin_of(step, way):
        return at_place(place - step if way == UP else place + step)

    def slab(origin, step, c, way, act):
        peer = at_place(place + 1 if way == UP else place - 1)

        def copy(columns):
            at = pl.ds(pl.multiple_of(origin * agg + c * chunk, chunk), chunk)
            act(pltpu.make_async_remote_copy(
                src_ref=slabs.at[at, pl.ds(0, columns)], dst_ref=slabs.at[at, pl.ds(0, columns)],
                send_sem=slab_send_sem.at[way, step, c], recv_sem=slab_recv_sem.at[way, step, c],
                device_id=(grp, peer), device_id_type=MESH,
            ))

        @pl.when(origin < line)
        def _():
            copy(kept)

        @pl.when(origin >= line)
        def _():
            copy(kept - agg)

    def start(copy):
        copy.start()

    def wait_send(copy):
        copy.wait_send()

    def wait_recv(copy):
        copy.wait_recv()

    def slab_open():
        def one(c, carry):
            for way in (UP, DOWN):
                slab(me, 0, c, way, start)
            return carry

        lax.fori_loop(0, CHUNKS, one, 0)

    events = (line - 1) * CHUNKS + halved

    def slab_passes(first, last):
        def one(event, carry):
            step = lax.div(event, CHUNKS)
            c = lax.rem(event, CHUNKS)
            for way in (UP, DOWN):
                at = c if way == UP else lax.rem(c + halved, CHUNKS)
                origin = origin_of(step + 1, way)
                slab(origin, step, at, way, wait_recv)

                @pl.when(event + CHUNKS < (line - 1) * CHUNKS + halved)
                def _():
                    slab(origin, step + 1, at, way, start)

            return carry

        lax.fori_loop(first, last, one, 0)

    def slab_close():
        def one(event, carry):
            step = lax.div(event, CHUNKS)
            c = lax.rem(event, CHUNKS)
            for way in (UP, DOWN):
                slab(origin_of(step, way), step, c if way == UP else lax.rem(c + halved, CHUNKS), way, wait_send)
            return carry

        lax.fori_loop(0, events, one, 0)

    half = parts // 2
    eye = iota((agg, agg), 0) == iota((agg, agg), 1)

    def take_slab(j):
        sl = aligned(j * agg, agg)
        cinv_ref[:, sl] = 1.0 / jnp.sum(jnp.where(eye, slabs[sl, :agg], 0.0), axis=0, keepdims=True)

        def place_tile(k):
            so = aligned(lax.rem(j + k, parts) * agg, agg)
            tile = slabs[sl, k * agg : (k + 1) * agg]
            m_hi[sl, so], m_lo[sl, so] = split(tile)
            if k:
                m_hi[so, sl], m_lo[so, sl] = split(tile.T)

        for k in range(half):
            place_tile(k)

        @pl.when(j < half)
        def _():
            place_tile(half)

    def take_slabs(first, last):
        def one(step, carry):
            take_slab(origin_of(step, UP))

            @pl.when(jnp.logical_and(step > 0, step < line))
            def _():
                take_slab(origin_of(step, DOWN))

            return carry

        lax.fori_loop(first, last, one, 0)

    slab_open()

    for d, slot in ((-1, 0), (1, 1)):
        @pl.when(jnp.logical_not(has[d]))
        def _():
            recv[:, slot] = jnp.zeros((recv.shape[0],) + recv.shape[2:], f32)
            r_recv[slot] = jnp.zeros(r_recv.shape[1:], f32)

    for d, slot in ((-2, 0), (2, 1)):
        @pl.when(jnp.logical_not(has[d]))
        def _():
            far[:, slot] = jnp.zeros((far.shape[0],) + far.shape[2:], f32)

    for ext in (ext_v, ext_w):
        ext[:ghost, :] = jnp.zeros((ghost, 2 * width), bf16)
        ext[ghost + rows_dev :, :] = jnp.zeros((ghost, 2 * width), bf16)
    for i in (1, 2, 4, 5, 0, 3):
        loads[i].wait()
    sent_row = jnp.concatenate([hi_ref[...], lo_ref[...]], axis=1).astype(f32)
    sent = jnp.broadcast_to(sent_row, (2 * ghost, 2 * ghost)).T.astype(jnp.int32)
    lane = iota((2 * ghost, block), 1)
    for j in range(blocks + 1):
        g_ref[: 2 * ghost, j * block : (j + 1) * block] = (sent + (ghost - j * block) == lane).astype(f32).astype(bf16)
    dinv_s[...] = jnp.zeros_like(dinv_s)
    oh_ref[:ghost, :] = jnp.zeros((ghost, agg), bf16)
    oh_ref[ghost + rows_dev :, :] = jnp.zeros((ghost, agg), bf16)
    sa[:, :block] = jnp.zeros((2 * ghost, block), f32)

    def fine(b):
        sl = aligned(b * block, block)
        low, high = band_tile(fv_ref, col_ref, b, block)
        diag = jnp.broadcast_to(fv_ref[0:1, sl], (block, block)).T
        dinv = 1.0 / diag
        diag_ref[sl, :] = diag
        dinv_ref[sl, :] = dinv
        for at, tile in ((0, low), (block, high)):
            hi, lo = split(tile)
            a2[aligned(b * 2 * block, block), at : at + block] = hi
            a2[aligned(b * 2 * block + block, block), at : at + block] = lo
        rhs = rhs_ref[sl, :]
        res_ref[sl, :] = rhs
        sol_ref[sl, :] = jnp.zeros_like(rhs)
        v = dinv * rhs
        xs[sl, :] = v
        ext_v[pl.ds(pl.multiple_of(ghost + b * block, ghost), block), :] = split_lanes(v)

    def setup(i, carry):
        for u in range(2):
            fine(2 * i + u)
        slab_passes(jnp.clip(i - FIRST, 0, events), jnp.clip(i + 1 - FIRST, 0, events))
        return carry

    lax.fori_loop(0, blocks // 2, setup, 0)
    done = min(blocks // 2 - FIRST, events)
    ends = [done] + [min(done + n, events) for n in (0, 2, 3, 5)]

    def sent_rows(b, carry):
        sl = aligned(b * block, block)
        onehot = (iota((agg, block), 0) == agg_ref[:, sl]).astype(f32)
        oht_ref[:, sl] = onehot.astype(bf16)
        oh_ref[pl.ds(pl.multiple_of(ghost + b * block, ghost), block), :] = onehot.T.astype(bf16)
        picked = (sent - b * block == lane).astype(f32).astype(bf16)
        both = dot(picked, a2[aligned(b * 2 * block, block), :]) + dot(picked, a2[aligned(b * 2 * block + block, block), :])
        sa[:, sl] = sa[:, sl] + both[:, :block]
        sa[:, aligned((b + 1) * block, block)] = both[:, block:]
        both = dot(picked, split_lanes(dinv_ref[sl, :]))
        dinv_s[...] += both[:, :block] + both[:, block:]
        return carry

    lax.fori_loop(0, blocks, sent_rows, 0, unroll=4)
    slab_passes(ends[0], ends[1])
    for j in range(blocks + 1):
        at = slice(j * block, (j + 1) * block)
        scaled = sa[:, at] * dinv_s[...]
        g_ref[2 * ghost : 4 * ghost, at], g_ref[4 * ghost :, at] = split(scaled)
        if j == 0:
            below = scaled
    spread_sent = dot(g_ref[...], oh_ref[...])
    go_ref[: 2 * ghost] = spread_sent[: 2 * ghost].astype(bf16)
    go_ref[2 * ghost : 4 * ghost], go_ref[4 * ghost :] = split(spread_sent[2 * ghost : 4 * ghost] + spread_sent[4 * ghost :])
    response = jnp.where(lane < ghost, below, scaled)
    r_send[0] = response[:ghost]
    r_send[1] = response[ghost:]

    def r_copy(way):
        d = (1, -1)[way]
        return pltpu.make_async_remote_copy(
            src_ref=r_send.at[way], dst_ref=r_recv.at[way],
            send_sem=r_send_sem.at[way], recv_sem=r_recv_sem.at[way],
            device_id=device(part + d), device_id_type=MESH,
        )

    def near_copy(ex, way, count):
        d = (1, -1)[way]
        return pltpu.make_async_remote_copy(
            src_ref=send.at[ex, way, pl.ds(0, count)], dst_ref=recv.at[ex, way, pl.ds(0, count)],
            send_sem=send_sem.at[ex, way], recv_sem=recv_sem.at[ex, way],
            device_id=device(part + d), device_id_type=MESH,
        )

    def far_copy(ex, way):
        d = (2, -2)[way]
        return pltpu.make_async_remote_copy(
            src_ref=send.at[ex, way, pl.ds(0, ghost)], dst_ref=far.at[ex, way],
            send_sem=far_send_sem.at[ex, way], recv_sem=far_recv_sem.at[ex, way],
            device_id=device(part + d), device_id_type=MESH,
        )

    def mid_product(double):
        high = 6 * ghost if double else 2 * ghost
        inner = slice(2 * block, (blocks - 1) * block)
        y_mid[:high] = dot(g_ref[:high, inner], ext_v[inner, :])

    def all_sent(double):
        high = 6 * ghost if double else 2 * ghost
        y = y_mid[:high]
        for rim in (slice(0, 2 * block), slice((blocks - 1) * block, (blocks + 1) * block)):
            y = y + dot(g_ref[:high, rim], ext_v[rim, :])
        return y

    def depart(ex, double, alpha, beta, y):
        now = y[: 2 * ghost, :width] + y[: 2 * ghost, width:]
        for way in range(2):
            send[ex, way, :ghost] = now[way * ghost : (way + 1) * ghost]
        if double:
            later = alpha * now - beta * quads(y[2 * ghost :], 2 * ghost, width)
            for way in range(2):
                send[ex, way, ghost:] = later[way * ghost : (way + 1) * ghost]
        for way, d in ((0, 1), (1, -1)):
            @pl.when(has[d])
            def _():
                near_copy(ex, way, 2 * ghost if double else ghost).start()
        if double:
            for way, d in ((0, 2), (1, -2)):
                @pl.when(has[d])
                def _():
                    far_copy(ex, way).start()

    def arrive(ex, double):
        count = 2 * ghost if double else ghost
        for way, d in ((0, -1), (1, 1)):
            @pl.when(has[d])
            def _():
                near_copy(ex, way, count).wait_recv()
                near_copy(ex, 1 - way, count).wait_send()

        if double:
            for way, d in ((0, -2), (1, 2)):
                @pl.when(has[d])
                def _():
                    far_copy(ex, way).wait_recv()
                    far_copy(ex, 1 - way).wait_send()

    def local_apply(ext, fn):
        def go(b, carry):
            a = a2[aligned(b * 2 * block, 2 * block), :]
            x = ext[pl.ds(pl.multiple_of(b * block, block), 2 * block), :]
            fn(b, aligned(b * block, block), quads(dot(a, x), block, width))
            return carry

        lax.fori_loop(0, blocks, go, 0, unroll=8)

    def store_ext(ext, b, x):
        ext[pl.ds(pl.multiple_of(ghost + b * block, ghost), block), :] = split_lanes(x)

    last_tile = (blocks - 1) * 2 * block
    below_rows = slice(0, ghost)
    above_rows = slice(rows_dev - ghost, rows_dev)

    def ghost_terms(ex):
        nothing = jnp.zeros((ghost, 2 * width), bf16)
        a_below = jnp.concatenate([a2[:ghost, :block], a2[block : block + ghost, :block]], axis=0)
        a_above = jnp.concatenate(
            [a2[last_tile + ghost : last_tile + block, block:], a2[last_tile + block + ghost : last_tile + 2 * block, block:]],
            axis=0,
        )
        from_below = jnp.concatenate([split_lanes(recv[ex, 0, :ghost]), nothing], axis=0)
        from_above = jnp.concatenate([nothing, split_lanes(recv[ex, 1, :ghost])], axis=0)
        return quads(dot(a_below, from_below), ghost, width), quads(dot(a_above, from_above), ghost, width)

    def pair(ex, te):
        alpha, beta = (1.0 - OMEGA, OMEGA) if te else (C1, C2)
        gamma = OMEGA if te else C2 - 1.0
        if not te:
            depart(ex, True, alpha, beta, all_sent(True))

        def first(b, sl, off):
            v = xs[sl, :]
            w = alpha * v - beta * (dinv_ref[sl, :] * off)
            store_ext(ext_w, b, w)
            r = res_ref[sl, :]
            if te:
                res_ref[sl, :] = r - alpha * (diag_ref[sl, :] * v) + gamma * off
                sol_ref[sl, :] += w
            else:
                res_ref[sl, :] = gamma * off - alpha * r
                sol_ref[sl, :] += v + w

        local_apply(ext_v, first)
        if not te:
            @pl.when(ex == 0)
            def _():
                slab_passes(ends[1], ends[2])

        def second(b, sl, off):
            r = res_ref[sl, :] - off
            res_ref[sl, :] = r
            v = dinv_ref[sl, :] * r
            xs[sl, :] = v
            store_ext(ext_v, b, v)

        local_apply(ext_w, second)
        mid_product(True)
        if not te:
            @pl.when(ex == 0)
            def _():
                slab_passes(ends[2], ends[3])
                take_slabs(0, min(2, ends[3] // CHUNKS + 1))

        arrive(ex, True)
        off_below, off_above = ghost_terms(ex)
        dw_below = -beta * (dinv_ref[below_rows, :] * off_below)
        dw_above = -beta * (dinv_ref[above_rows, :] * off_above)
        seen_below = jnp.concatenate([split_lanes(far[ex, 0]), split_lanes(send[ex, 1, :ghost])], axis=0)
        seen_above = jnp.concatenate([split_lanes(send[ex, 0, :ghost]), split_lanes(far[ex, 1])], axis=0)
        next_below = recv[ex, 0, ghost:] - beta * quads(dot(r2[0], seen_below), ghost, width)
        next_above = recv[ex, 1, ghost:] - beta * quads(dot(r2[1], seen_above), ghost, width)
        add_below = jnp.concatenate([split_lanes(next_below), split_lanes(dw_below)], axis=0)
        add_above = jnp.concatenate([split_lanes(dw_above), split_lanes(next_above)], axis=0)
        more_below = quads(dot(a2[: 2 * block, :block], add_below), block, width)
        more_above = quads(dot(a2[last_tile:, block:], add_above), block, width)
        zero = jnp.zeros((ghost, width), f32)
        dr_below = jnp.concatenate([gamma * off_below, zero], axis=0) - more_below
        dr_above = jnp.concatenate([zero, gamma * off_above], axis=0) - more_above
        sol_ref[below_rows, :] += dw_below
        sol_ref[above_rows, :] += dw_above
        for b, dr in ((0, dr_below), (blocks - 1, dr_above)):
            sl = slice(b * block, (b + 1) * block)
            r = res_ref[sl, :] + dr
            res_ref[sl, :] = r
            v = dinv_ref[sl, :] * r
            xs[sl, :] = v
            ext_v[ghost + b * block : ghost + (b + 1) * block, :] = split_lanes(v)

    def restricted(ex):
        depart(ex, False, 0.0, 0.0, all_sent(False))

        def restrict(b, sl, off):
            s2[sl, :] = split_lanes((1.0 - OMEGA) * res_ref[sl, :] - OMEGA * off)

        local_apply(ext_v, restrict)
        both = dot(oht_ref[...], s2[...])

        @pl.when(ex == 1)
        def _():
            slab_passes(ends[3], ends[4])
            taken = min(2, ends[3] // CHUNKS + 1)
            take_slabs(taken, max(taken, min(3, ends[4] // CHUNKS + 1)))

        arrive(ex, False)
        off_below, off_above = ghost_terms(ex)
        nothing = jnp.zeros((ghost, 2 * width), bf16)
        ds_below = jnp.concatenate([split_lanes(-OMEGA * off_below), nothing], axis=0)
        ds_above = jnp.concatenate([nothing, split_lanes(-OMEGA * off_above)], axis=0)
        both = both + dot(oht_ref[:, :block], ds_below) + dot(oht_ref[:, rows_dev - block :], ds_above)
        return both[:, :width] + both[:, width:]

    def polynomial():
        cinv = [cinv_ref[:, j * agg : (j + 1) * agg] for j in range(parts)]
        first_rho = 1.0 / (2.0 * THETA / DELTA - RHO0)
        mine_diag = own_ref[:, mine]
        mine_inv = 1.0 / jnp.sum(jnp.where(eye, mine_diag, 0.0), axis=1, keepdims=True)
        for j in range(parts):
            sl = slice(j * agg, (j + 1) * agg)
            begin = jnp.where(jnp.logical_and(eye, me == j), cinv[j], 0.0)
            z = begin - (mine_inv * own_ref[:, sl]) * cinv[j]
            d = first_rho * RHO0 * begin + (2.0 * first_rho / DELTA) * z
            pz[:, sl] = z
            pd[:, sl] = d
            px[:, sl] = begin + d
        rho_old = first_rho
        for turn in range(2, CHEB_COARSE):
            rho_new = 1.0 / (2.0 * THETA / DELTA - rho_old)
            hi, lo = split(pd[...])
            pair2[:agg, :] = hi
            pair2[agg:, :] = lo
            for j in range(parts // 2):
                sl = slice(2 * j * agg, (2 * j + 2) * agg)
                both = dot(pair2[...], m_hi[:, sl])
                low = dot(pair2[:agg, :], m_lo[:, sl])
                scale = jnp.concatenate([cinv[2 * j], cinv[2 * j + 1]], axis=1)
                z = pz[:, sl] - (both[:agg] + (both[agg:] + low)) * scale
                d = rho_new * rho_old * pd[:, sl] + (2.0 * rho_new / DELTA) * z
                pz[:, sl] = z
                pd[:, sl] = d
                px[:, sl] += d
            rho_old = rho_new
        hi, lo = split(px[...])
        m2[:agg, :] = hi
        m2[agg:, :] = lo

    pos = lax.div(me, 2)
    part_rows = agg // PIECES

    def coarse_copy(step, origin, c, peer, sends, recvs):
        at = pl.ds(pl.multiple_of(origin * agg + c * part_rows, part_rows), part_rows)
        return pltpu.make_async_remote_copy(
            src_ref=whole.at[step, at], dst_ref=whole.at[step, at], send_sem=sends, recv_sem=recvs,
            device_id=(grp, peer), device_id_type=MESH,
        )

    def along(step, far_by, way, c, origin):
        peer = me + 2 * far_by if way == UP else me - 2 * far_by
        return coarse_copy(step, origin, c, peer, line_send.at[step, way, far_by - 1, c], line_recv.at[step, way, far_by - 1, c])

    def over(step, c, origin):
        q = lax.div(origin, 2)
        return coarse_copy(step, origin, c, partner, over_send.at[step, q, c], over_recv.at[step, q, c])

    def reaches(far_by, way):
        return pos + far_by < line if way == UP else pos - far_by >= 0

    def gather_open(step):
        for c in range(PIECES):
            over(step, c, me).start()
            for far_by in reversed(range(1, line)):
                for way in (UP, DOWN):
                    @pl.when(reaches(far_by, way))
                    def _():
                        along(step, far_by, way, c, me).start()

    def gather_pass(step):
        for far_by in range(1, line):
            for c in range(PIECES):
                for way in (UP, DOWN):
                    @pl.when(reaches(far_by, 1 - way))
                    def _():
                        origin = me - 2 * far_by if way == UP else me + 2 * far_by
                        along(step, far_by, way, c, origin).wait_recv()
                        over(step, c, origin).start()

    def gather_close(step):
        for c in range(PIECES):
            for q in range(line):
                over(step, c, 2 * q + 1 - odd).wait_recv()
                over(step, c, 2 * q + odd).wait_send()
            for far_by in range(1, line):
                for way in (UP, DOWN):
                    @pl.when(reaches(far_by, way))
                    def _():
                        along(step, far_by, way, c, me).wait_send()

    for way, d in ((0, 1), (1, -1)):
        @pl.when(has[d])
        def _():
            r_copy(way).start()
    mid_product(True)

    def cycle_body(cycle, carry):
        ex = cycle * ROUNDS

        @pl.when(cycle == 0)
        def _():
            for way, d in ((0, 1), (1, -1)):
                @pl.when(has[-d])
                def _():
                    r_copy(way).wait_recv()

                @pl.when(has[d])
                def _():
                    r_copy(way).wait_send()

                hi, lo = split(r_recv[way])
                r2[way, :ghost] = hi
                r2[way, ghost:] = lo

        pair(ex, False)
        whole[cycle, mine, :] = restricted(ex + 1)
        gather_open(cycle)

        gather_pass(cycle)

        @pl.when(cycle == 0)
        def _():
            slab_passes(ends[4], events)
            slab_close()
            take_slabs(max(min(2, ends[3] // CHUNKS + 1), min(3, ends[4] // CHUNKS + 1)), line + 1)
            polynomial()

        gather_close(cycle)
        corr = split_lanes(quads(dot(m2[...], split_lanes(whole[cycle])), agg, width))
        depart(ex + 2, True, 1.0 - OMEGA, OMEGA, dot(go_ref[...], corr))

        def spread(b, c):
            sl = aligned(b * block, block)
            both = dot(oh_ref[pl.ds(pl.multiple_of(ghost + b * block, ghost), block), :], corr)
            t = both[:, :width] + both[:, width:]
            xs[sl, :] = t
            store_ext(ext_v, b, t)
            return c

        lax.fori_loop(0, blocks, spread, 0, unroll=4)
        pair(ex + 2, True)
        pair(ex + 3, False)
        return carry

    lax.fori_loop(0, CYCLES, cycle_body, 0)


def store_kernel(a_ref, b_ref, c_ref, d_ref, sem):
    copies = [pltpu.make_async_copy(a_ref, c_ref, sem.at[0]), pltpu.make_async_copy(b_ref, d_ref, sem.at[1])]
    for copy in copies:
        copy.start()
    for copy in copies:
        copy.wait()


def store(sol, res):
    return pl.pallas_call(
        store_kernel,
        in_specs=[pl.BlockSpec(memory_space=pltpu.VMEM)] * 2,
        out_specs=[pl.BlockSpec(memory_space=pltpu.HBM)] * 2,
        out_shape=[jax.ShapeDtypeStruct(sol.shape, f32)] * 2,
        scratch_shapes=[pltpu.SemaphoreType.DMA((2,))],
        name="store",
    )(*[pltpu.with_memory_space_constraint(x, pltpu.VMEM) for x in (sol, res)])


def body(n_grp, n_sub, right_side, fine_values, columns, agg_map, send_lo, send_hi, coarse_matrix):
    rows, width = right_side.shape
    ghost = send_lo.shape[0]
    block = 2 * ghost
    own = coarse_matrix[0]
    agg, coarse = own.shape
    kept = (coarse // agg // 2 + 1) * agg
    ext_rows = rows + block
    exchanges = CYCLES * ROUNDS
    vmem = pl.BlockSpec(memory_space=pltpu.VMEM)
    field = jax.ShapeDtypeStruct((rows, width), f32)
    dma = pltpu.SemaphoreType.DMA
    sol, res = pl.pallas_call(
        functools.partial(kernel, n_grp, n_sub),
        in_specs=[pl.BlockSpec(memory_space=pltpu.HBM)] * 7,
        out_specs=[vmem] * 2,
        out_shape=[field] * 2,
        scratch_shapes=[
            pltpu.VMEM((rows, width), f32),
            pltpu.VMEM(fine_values.shape, f32),
            pltpu.VMEM(columns.shape, jnp.int32),
            pltpu.VMEM((1, rows), jnp.int32),
            pltpu.VMEM((1, ghost), jnp.int32),
            pltpu.VMEM((1, ghost), jnp.int32),
            pltpu.VMEM((agg, coarse), f32),
            dma((7,)),
            pltpu.VMEM((2 * rows, 2 * block), bf16),
            pltpu.VMEM((rows, block), f32),
            pltpu.VMEM((rows, block), f32),
            pltpu.VMEM((ext_rows, agg), bf16),
            pltpu.VMEM((agg, rows), bf16),
            pltpu.VMEM((6 * ghost, ext_rows), bf16),
            pltpu.VMEM((2 * ghost, ext_rows), f32),
            pltpu.VMEM((2 * ghost, block), f32),
            pltpu.VMEM((rows, width), f32),
            pltpu.VMEM((ext_rows, 2 * width), bf16),
            pltpu.VMEM((ext_rows, 2 * width), bf16),
            pltpu.VMEM((rows, 2 * width), bf16),
            pltpu.VMEM((6 * ghost, 2 * width), f32),
            pltpu.VMEM((exchanges, 2, 2 * ghost, width), f32),
            pltpu.VMEM((exchanges, 2, 2 * ghost, width), f32),
            pltpu.VMEM((exchanges, 2, ghost, width), f32),
            pltpu.VMEM((2, ghost, 2 * ghost), f32),
            pltpu.VMEM((2, ghost, 2 * ghost), f32),
            pltpu.VMEM((2, 2 * ghost, 2 * ghost), bf16),
            dma((exchanges, 2)),
            dma((exchanges, 2)),
            dma((exchanges, 2)),
            dma((exchanges, 2)),
            dma((2,)),
            dma((2,)),
            pltpu.VMEM((coarse, kept), f32),
            dma((2, n_sub // 2, CHUNKS)),
            dma((2, n_sub // 2, CHUNKS)),
            pltpu.VMEM((1, coarse), f32),
            pltpu.VMEM((coarse, coarse), bf16),
            pltpu.VMEM((coarse, coarse), bf16),
            pltpu.VMEM((agg, coarse), f32),
            pltpu.VMEM((agg, coarse), f32),
            pltpu.VMEM((agg, coarse), f32),
            pltpu.VMEM((2 * agg, coarse), bf16),
            pltpu.VMEM((2 * agg, coarse), bf16),
            pltpu.VMEM((CYCLES, coarse, width), f32),
            dma((CYCLES, 2, n_sub // 2 - 1, PIECES)),
            dma((CYCLES, 2, n_sub // 2 - 1, PIECES)),
            dma((CYCLES, n_sub // 2, PIECES)),
            dma((CYCLES, n_sub // 2, PIECES)),
            pltpu.VMEM((6 * ghost, agg), bf16),
        ],
        compiler_params=pltpu.CompilerParams(
            collective_id=0, has_side_effects=True, vmem_limit_bytes=min(60 * 1024 * 1024, 27 * 1024 * 1024 + 9 * coarse * coarse)
        ),
        name="cycles",
    )(*[
        pltpu.with_memory_space_constraint(x, pltpu.HBM)
        for x in (right_side, fine_values, columns, agg_map.reshape(1, rows), send_lo.reshape(1, ghost), send_hi.reshape(1, ghost), own)
    ])
    return store(sol, res)


def solution(mesh):
    placed = (
        P(("grp", "sub"), None),
        P(None, ("grp", "sub")),
        P(None, ("grp", "sub")),
        P(("grp", "sub")),
        P(("grp", "sub")),
        P(("grp", "sub")),
        P("grp", "sub", None),
    )
    return jax.shard_map(
        functools.partial(body, mesh.shape["grp"], mesh.shape["sub"]),
        mesh=mesh,
        in_specs=placed,
        out_specs=(P(("grp", "sub"), None), P(("grp", "sub"), None)),
        check_vma=False,
    )
```
